256 devices in a mesh: seq: 16 (over x, y), chan: 16 (over z, core).
Axes of the slice: x: 4, y: 4, z: 8, core: 2. Of those that a mesh axis runs over, the one named last changes fastest.
Arguments:
- tokens: bfloat16 [16384, 4096], P('seq', 'chan'), may hold values from -6 to 6
- w_in: bfloat16 [4096, 4096], P(None, 'chan'), may hold values from -0.09375 to 0.09375
- residues: float32 [4096, 16], P('chan'), may hold values from -2.25 to 2.25
- decays: float32 [4096, 16], P('chan'), may hold values from 1.8310547e-05 to 2
- skip_gain: float32 [4096], P('chan'), may hold values from -1.2 to 1.2
- w_out: bfloat16 [4096, 4096], P('chan'), may hold values from -0.125 to 0.125
Outputs:
- mixed: bfloat16 [16384, 4096], P('seq', 'chan')
The draws below stay inside these ranges and needn't reach their ends.
All inputs are finite; a program needn't handle non-finite values.
Results may differ from the reference program's by a relative error of at most 0.03.
Values may be sent and summed in bfloat16 or wider, within the bound.
A program may use at most 128 MiB of HBM per device.

```python
import jax
import jax.numpy as jnp
from jax import lax

D = 4096
ORDER = 16
SEQ_LEN = 16384
N_CHAN = 16


def draw_decays(key, part):
    key = jax.random.fold_in(key, 11)
    key_base, key_ratio = jax.random.split(key, 2)
    paired = ORDER // 2
    low = jnp.log(0.3 / SEQ_LEN)
    high = jnp.log(2.0 / 1.5)
    base = jnp.exp(jax.random.uniform(key_base, (D, paired), jnp.float32, low, high))
    ratio = jnp.exp(jax.random.uniform(key_ratio, (D, paired), jnp.float32, jnp.log(1.2), jnp.log(1.5)))
    return jnp.stack([base, base * ratio], axis=2).reshape(D, ORDER)


def draw_residues(key, part):
    key = jax.random.fold_in(key, 13)
    key_mag, key_keep = jax.random.split(key)
    paired = ORDER // 2
    leading = 0.75 * jnp.clip(jax.random.normal(key_mag, (D, paired), jnp.float32), -3.0, 3.0)
    kept = jax.random.uniform(key_keep, (D, paired), jnp.float32, 0.5, 0.9)
    return jnp.stack([leading, -kept * leading], axis=2).reshape(D, ORDER)


def strengthened(array, rng, source, target, parts, factor):
    owner, partner = [(jnp.arange(array.shape[dim]) // (array.shape[dim] // parts)).reshape([-1 if axis == dim else 1 for axis in range(array.ndim)]) for dim in (source, target)]
    chosen = jax.random.permutation(rng, parts)[partner]
    strong = (owner == chosen) | (owner == (partner + parts // 2) % parts)
    return jnp.where(strong, factor * array, array)


def level_of(own_key, shape, cuts, low, high):
    loudness, own = 1.0, jax.random.fold_in(own_key, 6)
    for position, shards_of in cuts:
        heights = jnp.exp(jax.random.uniform(jax.random.fold_in(own, position), (shards_of,), jnp.float32, low / len(cuts), high / len(cuts)))
        loudness = loudness * jnp.repeat(heights, shape[position] // shards_of).reshape([-1 if axis == position else 1 for axis in range(len(shape))])
    return loudness


def bell_draw(own_key, shape, deviation, limit, cuts=(), kind=jnp.bfloat16):
    values = jax.random.normal(own_key, shape, jnp.float32) * deviation
    if len(cuts) > 0:
        values = level_of(own_key, shape, cuts, -0.22, 0.18) * values
    return jnp.clip(values, min=-limit, max=limit).astype(kind)


def bell_draw_with(stream_key, dims, deviation, bound, cuts, heavy, dtype=jnp.bfloat16):
    entries = deviation * jax.random.normal(stream_key, dims, jnp.float32)
    if cuts:
        entries = entries * level_of(stream_key, dims, cuts, -0.22, 0.18)
    return jnp.clip(strengthened(entries, jax.random.fold_in(stream_key, 3), *heavy), -bound, bound).astype(dtype)


def setup_inputs(seed: int = 0) -> dict:
    key_of = jax.random.split(jax.random.key(seed), 7)
    tokens = bell_draw(key_of[0], (SEQ_LEN, D), 1.0, 6.0, ((0, 16), (1, 16)))
    w_in = bell_draw(key_of[1], (D, D), D ** -0.5, 0.09375, ((1, 16),))
    residues = draw_residues(jax.random.fold_in(key_of[6], 71), 0)
    decays = draw_decays(jax.random.fold_in(key_of[6], 71), 0)
    skip_gain = bell_draw(key_of[4], (D,), 0.3, 1.2, ((0, 16),), jnp.float32)
    w_out = bell_draw_with(key_of[5], (D, D), D ** -0.5, 0.125, ((0, 16),), (0, 1, 16, 2.0))
    return {"tokens": tokens, "w_in": w_in, "residues": residues, "decays": decays, "skip_gain": skip_gain, "w_out": w_out}


def block_conv(blocks):
    stream_block, res_block, dec_block = blocks
    length = stream_block.shape[0]
    positions = jnp.arange(length).astype(jnp.float32)
    kernel = jnp.zeros(stream_block.shape, jnp.float32)
    for order_idx in range(ORDER):
        decay_rate = dec_block[:, order_idx]
        kernel = kernel + (res_block[:, order_idx] * jnp.sqrt(decay_rate))[None, :] * jnp.exp(-decay_rate[None, :] * positions[:, None])
    spectra = jnp.fft.rfft(stream_block.astype(jnp.float32), n=2 * length, axis=0) * jnp.fft.rfft(kernel, n=2 * length, axis=0)
    return jnp.fft.irfft(spectra, n=2 * length, axis=0)[:length].astype(jnp.float32)

def reference(tokens, w_in, residues, decays, skip_gain, w_out):
    stream = jnp.dot(tokens, w_in, preferred_element_type=jnp.float32).astype(jnp.bfloat16)
    width = stream.shape[1]
    block_width = 512 if width % 512 == 0 else width
    count = width // block_width
    grouped = stream.reshape(SEQ_LEN, count, block_width).transpose(1, 0, 2)
    long_part = lax.map(block_conv, (grouped, residues.reshape(count, block_width, ORDER), decays.reshape(count, block_width, ORDER)))
    long_part = long_part.transpose(1, 0, 2).reshape(SEQ_LEN, width)
    conv = (long_part + skip_gain[None, :] * stream.astype(jnp.float32)).astype(jnp.bfloat16)
    group_width = width // N_CHAN
    conv_groups = conv.reshape(SEQ_LEN, N_CHAN, group_width).transpose(1, 0, 2)
    weight_groups = w_out.reshape(N_CHAN, group_width, width)

    def add_group(total, pieces):
        term = jnp.dot(pieces[0], pieces[1], preferred_element_type=jnp.float32)
        rounded = lax.optimization_barrier(term.astype(jnp.bfloat16)).astype(jnp.float32)
        return (total + rounded, 0)
    mixed, _ = lax.scan(add_group, jnp.zeros((SEQ_LEN, width), jnp.float32), (conv_groups, weight_groups))
    return mixed.astype(jnp.bfloat16)
```

```python
import functools

import jax
import jax.numpy as jnp
from jax import lax
from jax.experimental import pallas as pl
from jax.experimental.pallas import tpu as pltpu
from jax.sharding import PartitionSpec as P

MESH = pl.DeviceIdType.MESH
F32 = jnp.float32
BF16 = jnp.bfloat16
SUB = 8
LANES = 128
PIECES = 8


def kernel(
    nseq, nz, rows, width, order,
    tokens, w_in, residues, decays, skip, w_out, out,
    x_buf, wi_buf, wo_buf, acc, u_buf, conv, part, arrived, leaving,
    g_buf, d_buf, power, before, total, states, carry_in,
    ring_in, ring_out, pair_in, pair_out, sum_in, sum_out, state_in, state_out, conv_in, conv_out,
    wo_in, wo_sent, local,
):
    row = lax.axis_index("seq")
    chan = lax.axis_index("chan")
    z, core = chan // 2, chan % 2
    step_dir = 1 - 2 * core
    up = lax.rem(z + step_dir + nz, nz)
    down = lax.rem(z - step_dir + nz, nz)
    next_dev = {"chan": 2 * up + core}
    prev_dev = {"chan": 2 * down + core}
    twin = {"chan": 2 * z + 1 - core}
    half = rows // 2
    piece = rows // PIECES
    per_half = PIECES // 2
    span = half // SUB
    tiles = width // LANES

    barrier = pltpu.get_barrier_semaphore()
    for other in (next_dev, prev_dev, twin):
        pl.semaphore_signal(barrier, inc=1, device_id=other, device_id_type=MESH)

    def greet(step, _):
        other = lax.rem(row + step, nseq)
        pl.semaphore_signal(barrier, inc=1, device_id={"seq": other}, device_id_type=MESH)
        return 0

    lax.fori_loop(1, nseq, greet, 0)
    own_tokens = pltpu.make_async_copy(tokens, x_buf.at[chan], local.at[0])
    own_tokens.start()
    load_wi = pltpu.make_async_copy(w_in, wi_buf, local.at[1])
    load_wi.start()
    pl.semaphore_wait(barrier, nseq + 2)

    def block_of(step):
        mine = lax.rem(z - step_dir * step + 2 * nz, nz)
        theirs = lax.rem(z + step_dir * step + 2 * nz, nz)
        return 2 * mine + core, 2 * theirs + 1 - core

    def ring_copy(step, p, src_block, src=None):
        rows_p = pl.ds(p * piece, piece)
        src = x_buf.at[src_block, rows_p] if src is None else src.at[rows_p]
        return pltpu.make_async_remote_copy(
            src_ref=src, dst_ref=x_buf.at[src_block, rows_p],
            send_sem=ring_out.at[step, p], recv_sem=ring_in.at[step, p],
            device_id=next_dev, device_id_type=MESH)

    def pair_copy(step, p, src_block, src=None):
        rows_p = pl.ds(p * piece, piece)
        src = x_buf.at[src_block, rows_p] if src is None else src.at[rows_p]
        return pltpu.make_async_remote_copy(
            src_ref=src, dst_ref=x_buf.at[src_block, rows_p],
            send_sem=pair_out.at[step, p], recv_sem=pair_in.at[step, p],
            device_id=twin, device_id_type=MESH)

    def wo_copy(block):
        cols = pl.ds(pl.multiple_of((2 * block + 1 - core) * width, LANES), width)
        return pltpu.make_async_remote_copy(
            src_ref=w_out.at[:, cols], dst_ref=wo_buf.at[block, pl.ds(core * width, width)],
            send_sem=wo_sent.at[block], recv_sem=wo_in.at[block],
            device_id=twin, device_id_type=MESH)

    def wo_load(block):
        cols = pl.ds(pl.multiple_of((2 * block + core) * width, LANES), width)
        return pltpu.make_async_copy(
            w_out.at[:, cols], wo_buf.at[block, pl.ds(core * width, width)], local.at[2 + block])

    for p in range(per_half):
        ring_copy(0, p, chan, tokens).start()
    for p in range(per_half):
        pair_copy(0, p, chan, tokens).start()

    gain = residues[...] * jnp.sqrt(decays[...])
    g_buf[...] = gain.T
    d_buf[...] = decays[...].T
    place = lax.broadcasted_iota(jnp.int32, (SUB, width), 0).astype(F32)
    for r in range(order):
        power[r] = jnp.exp(-d_buf[r:r + 1] * (place * span))

    own_tokens.wait()
    load_wi.wait()

    def project(h, step, first):
        mine, theirs = block_of(step)
        rows_h = pl.ds(h * half, half)
        term = jnp.dot(x_buf[mine, rows_h], wi_buf[mine], preferred_element_type=F32)
        term += jnp.dot(x_buf[theirs, rows_h], wi_buf[theirs], preferred_element_type=F32)
        if first:
            acc[rows_h] = term
        else:
            acc[rows_h] += term

    def pair_wait(h, step):
        _, theirs = block_of(step)
        for p in range(h * per_half, (h + 1) * per_half):
            pair_copy(step, p, theirs).wait_recv()

    def ring_step(h, step):
        mine, _ = block_of(step)
        for p in range(h * per_half, (h + 1) * per_half):
            ring_copy(step - 1, p, mine).wait_recv()
            ring_copy(step, p, mine).start()
            pair_copy(step, p, mine).start()
        pair_wait(h, step)
        project(h, step, False)

    def last_step(h):
        mine, _ = block_of(nz - 1)
        for p in range(h * per_half, (h + 1) * per_half):
            ring_copy(nz - 2, p, mine).wait_recv()
            pair_copy(nz - 1, p, mine).start()
        pair_wait(h, nz - 1)
        project(h, nz - 1, False)
        rows_h = pl.ds(h * half, half)
        for tile in range(tiles):
            u_buf[tile, rows_h] = acc[rows_h, tile * LANES:(tile + 1) * LANES].astype(BF16).astype(F32)

    def steps(h, first, last):
        def body(step, _):
            ring_step(h, step)
            return 0
        lax.fori_loop(first, last, body, 0)

    def scan(h, tile):
        lanes = pl.ds(tile * LANES, LANES)
        a = [jnp.broadcast_to(jnp.exp(-d_buf[r:r + 1, lanes]), (SUB, LANES)) for r in range(order)]
        g = [jnp.broadcast_to(g_buf[r:r + 1, lanes], (SUB, LANES)) for r in range(order)]
        direct = jnp.broadcast_to(skip[:, lanes], (SUB, LANES))

        def body(i, hs):
            where = pl.ds(h * half + i, SUB, stride=span)
            u = u_buf[tile, where]
            hs = tuple(a[r] * hs[r] + g[r] * u for r in range(order))
            terms = [direct * u] + list(hs)
            while len(terms) > 1:
                terms = [terms[k] + terms[k + 1] if k + 1 < len(terms) else terms[k] for k in range(0, len(terms), 2)]
            u_buf[tile, where] = terms[0]
            return hs

        hs = lax.fori_loop(0, span, body, tuple(jnp.zeros((SUB, LANES), F32) for _ in range(order)))
        sub = lax.broadcasted_iota(jnp.int32, (SUB, LANES), 0)
        for r in range(order):
            run = hs[r]
            for shift in (1, 2, 4):
                factor = jnp.exp(-d_buf[r:r + 1, lanes] * float(span * shift))
                run = run + jnp.where(sub >= shift, factor * pltpu.roll(run, shift, 0), 0.0)
            before[h, r, :, lanes] = jnp.where(sub >= 1, pltpu.roll(run, 1, 0), 0.0)
            total[h, r:r + 1, lanes] = run[SUB - 1:SUB]

    def finish(h, tile):
        lanes = pl.ds(tile * LANES, LANES)
        a = [jnp.broadcast_to(jnp.exp(-d_buf[r:r + 1, lanes]), (SUB, LANES)) for r in range(order)]
        hs = tuple(
            before[h, r, :, lanes] + power[r, :, lanes] * carry_in[h, r:r + 1, lanes] for r in range(order))

        def body(i, hs):
            where = pl.ds(h * half + i, SUB, stride=span)
            hs = tuple(a[r] * hs[r] for r in range(order))
            terms = [u_buf[tile, where]] + list(hs)
            while len(terms) > 1:
                terms = [terms[k] + terms[k + 1] if k + 1 < len(terms) else terms[k] for k in range(0, len(terms), 2)]
            u_buf[tile, where] = terms[0]
            return hs

        lax.fori_loop(0, span, body, hs)

    pair_wait(0, 0)
    project(0, 0, True)
    steps(0, 1, nz - 1)
    for p in range(per_half, PIECES):
        ring_copy(0, p, chan, tokens).start()
    for p in range(per_half, PIECES):
        pair_copy(0, p, chan, tokens).start()
    last_step(0)
    pair_wait(1, 0)
    project(1, 0, True)
    for block in range(nz):
        wo_load(block).start()
        wo_copy(block).start()
    bounds = [1 + (k * (nz - 2)) // (tiles + 1) for k in range(tiles + 2)]
    for tile in range(tiles):
        steps(1, bounds[tile], bounds[tile + 1])
        scan(0, tile)
    steps(1, bounds[tiles], nz - 1)
    last_step(1)

    for tile in range(tiles):
        scan(1, tile)
    half_decay = jnp.exp(-d_buf[...] * float(half))
    states[row] = half_decay * total[0] + total[1]

    def state_copy(src, target):
        return pltpu.make_async_remote_copy(
            src_ref=states.at[src], dst_ref=states.at[src],
            send_sem=state_out.at[target], recv_sem=state_in.at[src],
            device_id={"seq": target}, device_id_type=MESH)

    def send_state(target, _):
        state_copy(row, target).start()
        return 0

    lax.fori_loop(row + 1, nseq, send_state, 0)
    block_decay = jnp.exp(-d_buf[...] * float(rows))

    def add_state(src, carry):
        state_copy(src, row).wait_recv()
        return block_decay * carry + states[src]

    carry = lax.fori_loop(0, row, add_state, jnp.zeros((order, width), F32))
    carry_in[0] = carry
    carry_in[1] = half_decay * carry + total[0]

    def conv_copy(h):
        rows_h = pl.ds(h * half, half)
        return pltpu.make_async_remote_copy(
            src_ref=conv.at[core, rows_h], dst_ref=conv.at[core, rows_h],
            send_sem=conv_out.at[h], recv_sem=conv_in.at[h], device_id=twin, device_id_type=MESH)

    def conv_from_twin(h):
        rows_h = pl.ds(h * half, half)
        return pltpu.make_async_remote_copy(
            src_ref=conv.at[1 - core, rows_h], dst_ref=conv.at[1 - core, rows_h],
            send_sem=conv_out.at[h], recv_sem=conv_in.at[h], device_id=twin, device_id_type=MESH)

    for h in range(2):
        for tile in range(tiles):
            finish(h, tile)
        rows_h = pl.ds(h * half, half)
        for tile in range(tiles):
            conv[core, rows_h, pl.ds(tile * LANES, LANES)] = u_buf[tile, rows_h].astype(BF16)
        conv_copy(h).start()

    for block in range(nz):
        wo_load(block).wait()
        wo_copy(block).wait_recv()

    def own_part(step, h):
        block = lax.rem(z - step_dir * (step + 1) + 2 * nz, nz)
        rows_h = pl.ds(h * half, half)
        part[rows_h] = jnp.dot(
            conv[0, rows_h], wo_buf[block, :width], preferred_element_type=F32) + jnp.dot(
            conv[1, rows_h], wo_buf[block, width:], preferred_element_type=F32)

    def sum_copy(step, p):
        rows_p = pl.ds(p * piece, piece)
        return pltpu.make_async_remote_copy(
            src_ref=leaving.at[step, rows_p], dst_ref=arrived.at[step, rows_p],
            send_sem=sum_out.at[step, p], recv_sem=sum_in.at[step, p],
            device_id=next_dev, device_id_type=MESH)

    for h in range(2):
        conv_from_twin(h).wait_recv()
        own_part(0, h)
        for p in range(h * per_half, (h + 1) * per_half):
            rows_p = pl.ds(p * piece, piece)
            leaving[0, rows_p] = part[rows_p].astype(BF16)
            sum_copy(0, p).start()

    def sum_step(step, _):
        for h in range(2):
            own_part(step, h)
        for p in range(PIECES):
            rows_p = pl.ds(p * piece, piece)
            sum_copy(step - 1, p).wait_recv()
            leaving[step, rows_p] = (arrived[step - 1, rows_p].astype(F32) + part[rows_p]).astype(BF16)
            sum_copy(step, p).start()
        return 0

    lax.fori_loop(1, nz - 1, sum_step, 0)
    for h in range(2):
        own_part(nz - 1, h)
    for p in range(PIECES):
        rows_p = pl.ds(p * piece, piece)
        sum_copy(nz - 2, p).wait_recv()
        out[rows_p] = (arrived[nz - 2, rows_p].astype(F32) + part[rows_p]).astype(BF16)

    def drain(step, _):
        for p in range(PIECES):
            ring_copy(step, p, chan).wait_send()
            pair_copy(step, p, chan).wait_send()
            sum_copy(step, p).wait_send()
        return 0

    lax.fori_loop(0, nz - 1, drain, 0)
    for p in range(PIECES):
        pair_copy(nz - 1, p, chan).wait_send()
    for block in range(nz):
        wo_copy(block).wait_send()
    for h in range(2):
        conv_copy(h).wait_send()

    def drain_state(target, _):
        state_copy(row, target).wait_send()
        return 0

    lax.fori_loop(row + 1, nseq, drain_state, 0)


def per_device(nseq, nchan, tokens, w_in, residues, decays, skip_gain, w_out):
    rows, width = tokens.shape
    order = residues.shape[1]
    nz = nchan // 2
    dma = pltpu.SemaphoreType.DMA
    vmem = pl.BlockSpec(memory_space=pltpu.VMEM)
    hbm = pl.BlockSpec(memory_space=pl.ANY)
    flops = 4 * rows * width * nchan * width
    return pl.pallas_call(
        functools.partial(kernel, nseq, nz, rows, width, order),
        out_shape=jax.ShapeDtypeStruct((rows, width), BF16),
        in_specs=[hbm, hbm, vmem, vmem, vmem, hbm],
        out_specs=vmem,
        scratch_shapes=[
            pltpu.VMEM((nchan, rows, width), BF16),
            pltpu.VMEM((nchan, width, width), BF16),
            pltpu.VMEM((nz, 2 * width, width), BF16),
            pltpu.VMEM((rows, width), F32),
            pltpu.VMEM((width // LANES, rows, LANES), F32),
            pltpu.VMEM((2, rows, width), BF16),
            pltpu.VMEM((rows, width), F32),
            pltpu.VMEM((nz - 1, rows, width), BF16),
            pltpu.VMEM((nz - 1, rows, width), BF16),
            pltpu.VMEM((order, width), F32),
            pltpu.VMEM((order, width), F32),
            pltpu.VMEM((order, SUB, width), F32),
            pltpu.VMEM((2, order, SUB, width), F32),
            pltpu.VMEM((2, order, width), F32),
            pltpu.VMEM((nseq, order, width), F32),
            pltpu.VMEM((2, order, width), F32),
            dma((nz - 1, PIECES)), dma((nz - 1, PIECES)),
            dma((nz, PIECES)), dma((nz, PIECES)),
            dma((nz - 1, PIECES)), dma((nz - 1, PIECES)),
            dma((nseq,)), dma((nseq,)),
            dma((2,)), dma((2,)),
            dma((nz,)), dma((nz,)),
            dma((2 + nz,)),
        ],
        compiler_params=pltpu.CompilerParams(
            collective_id=0, has_side_effects=True, vmem_limit_bytes=48 * 1024 * 1024),
        cost_estimate=pl.CostEstimate(flops=flops, bytes_accessed=6 * 1024 * 1024, transcendentals=0),
    )(tokens, w_in.reshape(nchan, width, width), residues, decays, skip_gain.reshape(1, width), w_out)


def solution(mesh):
    in_specs = (
        P("seq", "chan"),
        P(None, "chan"),
        P("chan", None),
        P("chan", None),
        P("chan"),
        P("chan", None),
    )
    return jax.shard_map(
        functools.partial(per_device, mesh.shape["seq"], mesh.shape["chan"]),
        mesh=mesh, in_specs=in_specs, out_specs=P("seq", "chan"), check_vma=False)
```

```python
import functools

import jax
import jax.numpy as jnp
from jax import lax
from jax.experimental import pallas as pl
from jax.experimental.pallas import tpu as pltpu
from jax.sharding import PartitionSpec as P

MESH = pl.DeviceIdType.MESH
F32 = jnp.float32
BF16 = jnp.bfloat16
SUB = 8
LANES = 128
UNROLL = 8
LAG = 4
NX = 4
WI_FIRST, WI_SECOND, WO_START, WO_FIRST, WO_SECOND, WI_DONE = 3, 6, 6, 10, 13, 13


def hop_counts(nz):
    group = nz // 2
    up, down = {}, {}
    for r in range(nz):
        last = r + group - 1
        if r == 0:
            up[r], down[r] = last, 0
        elif last >= nz:
            up[r], down[r] = last - nz, nz - r
        elif last < nz - r:
            up[r], down[r] = last, 0
        else:
            up[r], down[r] = 0, nz - r
    return up, down


def schedule(lengths):
    left = {r: n for r, n in lengths.items() if n > 0}
    ready = {r: 0 for r in left}
    items, place = [], 0
    while left:
        able = [r for r in left if ready[r] <= place]
        if able:
            r = max(able, key=lambda r: (left[r], -r))
            items.append((r, lengths[r] - left[r] + 1))
            left[r] -= 1
            ready[r] = place + LAG
            if left[r] == 0:
                del left[r]
        place += 1
    return items


def paths(nz):
    up, down = hop_counts(nz)
    first = schedule(up)
    mirror = {r: (nz // 2 + 1 - r) % nz for r in range(nz)}
    second = [(mirror[r], h) for r, h in first]
    assert sorted(second) == sorted((r, h) for r in down for h in range(1, down[r] + 1))
    return up, down, (first, second)


def kernel(
    nseq, nz, rows, width, order,
    tokens, w_in, residues, decays, skip, w_out, out,
    x_buf, relay, wi_a, wi_b, wo_a, wo_b, acc, u_buf, conv, part, arrived, leaving,
    far_res, far_dec, far_skip, g_buf, d_buf, k_buf, power, before, last, tail, states, carries, pair_last,
    ring_in, ring_out, pair_in, pair_out, own_in, own_out, sum_in, sum_out, state_in, state_out, conv_in, conv_out,
    wo_in, wo_sent, far_in, far_out, line_in, line_out, prm_in, prm_out, join_in, join_out, local,
):
    row = lax.axis_index("seq")
    chan = lax.axis_index("chan")
    z, core = chan // 2, chan % 2
    ny = nseq // NX
    x, y = row // ny, row % ny
    group = nz // 2
    sub = rows // nz
    mine = group * sub
    span = mine // SUB
    wide = 2 * width
    tiles = wide // LANES
    per_slot = SUB // group
    up, down, lists = paths(nz)
    count = len(lists[0])
    index = [{item: n for n, item in enumerate(items)} for items in lists]
    way = (1, -1)

    def at(dz, c):
        return {"chan": 2 * lax.rem(z + dz + nz, nz) + c}

    ring_dev = [at(1, core), at(nz - 1, core)]
    twin = at(0, 1 - core)
    partner = at(group, core)
    across = at(group, 1 - core)

    barrier = pltpu.get_barrier_semaphore()
    for other in (ring_dev[0], ring_dev[1], twin, partner, across):
        pl.semaphore_signal(barrier, inc=1, device_id=other, device_id_type=MESH)

    def greet(step, _):
        pl.semaphore_signal(
            barrier, inc=1, device_id={"seq": lax.rem(row + step, nseq)}, device_id_type=MESH)
        return 0

    lax.fori_loop(1, nseq, greet, 0)

    def remote(src, dst, send, recv, device):
        return pltpu.make_async_remote_copy(
            src_ref=src, dst_ref=dst, send_sem=send, recv_sem=recv, device_id=device, device_id_type=MESH)

    def slot_of(side, r, h):
        j = (way[side] * h - r) % nz
        return group - 1 - j if j < group else None

    def source_block(side, h, c):
        return 2 * lax.rem(z - way[side] * h + 2 * nz, nz) + c

    def slot_rows(k):
        return pl.ds(k * sub, sub)

    relays = [[item for item in lists[side] if slot_of(side, *item) is None] for side in (0, 1)]

    def place_of(side, r, h, block):
        k = slot_of(side, r, h)
        if k is None:
            return relay.at[side, relays[side].index((r, h))]
        return x_buf.at[block, slot_rows(k)]

    def own_rows(r):
        q = lax.rem(z + r, nz)
        return pl.ds(pl.multiple_of(q * sub, sub), sub)

    def ring_copy(side, r, h):
        block = source_block(side, h - 1, core)
        src = tokens.at[own_rows(r)] if h == 1 else place_of(side, r, h - 1, block)
        n = index[side][(r, h)]
        return remote(src, place_of(side, r, h, block), ring_out.at[side, n], ring_in.at[side, n], ring_dev[side])

    def pair_copy(side, r, h, from_twin=False):
        block = source_block(side, h, 1 - core if from_twin else core)
        ref = place_of(side, r, h, block)
        n = index[side][(r, h)]
        return remote(ref, ref, pair_out.at[side, n], pair_in.at[side, n], twin)

    own_parts = [r for r in range(nz) if (-r) % nz < group]

    def own_slot(r):
        return group - 1 - (-r) % nz

    def own_load(n):
        r = own_parts[n]
        return pltpu.make_async_copy(
            tokens.at[own_rows(r)], x_buf.at[chan, slot_rows(own_slot(r))], local.at[n])

    def own_pair(n):
        r = own_parts[n]
        return remote(
            tokens.at[own_rows(r)], x_buf.at[chan, slot_rows(own_slot(r))], own_out.at[n], own_in.at[n], twin)

    wi_load = pltpu.make_async_copy(w_in, wi_a, local.at[group])

    far_wi = remote(w_in.at[row], wi_b.at[x, y], far_out.at[0], far_in.at[0], partner)

    def far_wo(c):
        cols = pl.ds(pl.multiple_of((2 * (row // 2) + c) * width, LANES), width)
        device = {"chan": 2 * lax.rem(z + group, nz) + c}
        return remote(w_out.at[:, cols], wo_b.at[x, y], far_out.at[1 + c], far_in.at[1], device)

    def lines(which, stage):
        buf = (wi_b, wo_b)[which]
        low, high = pl.ds(0, width // 2), pl.ds(width // 2, width // 2)
        copies = []
        for step in range(1, NX):
            n = (step - 1, which, stage)
            device = {"seq": lax.rem(x + step, NX) * ny + y}
            ref = buf.at[x, y, low] if stage == 0 else buf.at[x, :, high]
            copies.append(remote(ref, ref, line_out.at[n], line_in.at[n], device))
        for step in range(1, ny):
            n = (NX - 1 + step - 1, which, stage)
            device = {"seq": x * ny + lax.rem(y + step, ny)}
            ref = buf.at[x, y, high] if stage == 0 else buf.at[:, y, low]
            copies.append(remote(ref, ref, line_out.at[n], line_in.at[n], device))
        return copies

    params = [
        remote(src, dst, prm_out.at[n], prm_in.at[n], partner)
        for n, (src, dst) in enumerate(((residues, far_res), (decays, far_dec), (skip, far_skip)))]

    def wo_cols(block, c):
        return pl.ds(pl.multiple_of((2 * block + c) * width, LANES), width)

    def wo_copy(block):
        return remote(
            w_out.at[:, wo_cols(block, 1 - core)], wo_a.at[block, pl.ds(core * width, width)],
            wo_sent.at[block], wo_in.at[block], twin)

    def wo_load(block):
        return pltpu.make_async_copy(
            w_out.at[:, wo_cols(block, core)], wo_a.at[block, pl.ds(core * width, width)],
            local.at[group + 1 + block])

    def project(delta, ab, first):
        total = None
        source = lax.rem(z - delta + nz, nz)
        for c in range(2):
            block = 2 * source + c
            weights = wi_a[block] if ab == 0 else wi_b[block // ny, lax.rem(block, ny)]
            term = jnp.dot(x_buf[block], weights, preferred_element_type=F32)
            total = term if total is None else total + term
        cols = pl.ds(ab * width, width)
        if first:
            acc[:, cols] = total
        else:
            acc[:, cols] += total

    for n in range(group):
        own_load(n).start()
    wi_load.start()
    pl.semaphore_wait(barrier, nseq + 4)
    far_wi.start()
    for side in (0, 1):
        ring_copy(side, *lists[side][0]).start()
    for copy in params:
        copy.start()
    for n in range(group):
        own_pair(n).start()

    sources = {}
    for side in (0, 1):
        for n, (r, h) in enumerate(lists[side]):
            if slot_of(side, r, h) is not None:
                sources.setdefault((way[side] * h) % nz, []).append((side, r, h, n))
    whole = {delta: max(n for _, _, _, n in got) + LAG + 1 for delta, got in sources.items()}

    arrived_items, fresh = set(), []

    def arrive(side, r, h):
        if (side, r, h) not in arrived_items:
            arrived_items.add((side, r, h))
            fresh.append((side, r, h))
            ring_copy(side, r, h).wait_recv()

    far_ready = False
    projected = []
    for step in range(max(count + LAG + 2, WI_DONE + 1)):
        for side in (0, 1):
            if 0 < step < count:
                r, h = lists[side][step]
                if h > 1:
                    arrive(side, r, h - 1)
                ring_copy(side, r, h).start()
        for side in (0, 1):
            if LAG <= step < count + LAG:
                arrive(side, *lists[side][step - LAG])
            for item in list(fresh):
                fresh.remove(item)
                if slot_of(*item) is not None:
                    pair_copy(*item).start()
        if step == 1:
            for block in range(nz):
                wo_load(block).start()
                wo_copy(block).start()
        if step == 2:
            for n in range(group):
                own_load(n).wait()
                own_pair(n).wait_recv()
            wi_load.wait()
            project(0, 0, True)
            projected.append(0)
        if step == WO_START:
            @pl.when(core == lax.rem(row, 2))
            def _():
                for c in range(2):
                    far_wo(c).start()
        if step == WI_FIRST:
            far_wi.wait_recv()
            for copy in lines(0, 0):
                copy.start()
        if step == WI_SECOND:
            for copy in lines(0, 0):
                copy.wait_recv()
            for copy in lines(0, 1):
                copy.start()
        if step == WO_FIRST:
            far_wo(0).wait_recv()
            for copy in lines(1, 0):
                copy.start()
        if step == WO_SECOND:
            for copy in lines(1, 0):
                copy.wait_recv()
            for copy in lines(1, 1):
                copy.start()
        if step == WI_DONE:
            for copy in lines(0, 1):
                copy.wait_recv()
            far_ready = True
            for n, delta in enumerate(projected):
                project(delta, 1, n == 0)
            for copy in params:
                copy.wait_recv()
            near, far = pl.ds(0, width), pl.ds(width, width)
            g_buf[:, near] = residues[...] * jnp.sqrt(decays[...])
            g_buf[:, far] = far_res[...] * jnp.sqrt(far_dec[...])
            d_buf[:, near] = decays[...]
            d_buf[:, far] = far_dec[...]
            k_buf[:, near] = skip[...]
            k_buf[:, far] = far_skip[...]
        for delta, ready in whole.items():
            if ready == step:
                for side, r, h, _ in sources[delta]:
                    pair_copy(side, r, h, True).wait_recv()
                project(delta, 0, False)
                if far_ready:
                    project(delta, 1, False)
                projected.append(delta)
    assert far_ready and len(projected) == nz
    for tile in range(tiles):
        u_buf[tile] = acc[:, tile * LANES:(tile + 1) * LANES].astype(BF16).astype(F32)

    low_chip = z < group
    cut = jnp.where(low_chip, per_slot * (group - 1 - z), 0)
    sub_id = lax.broadcasted_iota(jnp.int32, (SUB, LANES), 0)
    away = (sub_id - jnp.where(sub_id >= cut, cut, 0)).astype(F32) * float(span)

    def combine(terms):
        while len(terms) > 1:
            terms = [terms[k] + terms[k + 1] if k + 1 < len(terms) else terms[k] for k in range(0, len(terms), 2)]
        return terms[0]

    def scan(tile):
        lanes = pl.ds(tile * LANES, LANES)
        a = [jnp.broadcast_to(jnp.exp(-d_buf[r:r + 1, lanes]), (SUB, LANES)) for r in range(order)]
        g = [jnp.broadcast_to(g_buf[r:r + 1, lanes], (SUB, LANES)) for r in range(order)]
        direct = jnp.broadcast_to(k_buf[:, lanes], (SUB, LANES))

        def body(i, hs):
            where = pl.ds(i, SUB, stride=span)
            u = u_buf[tile, where]
            hs = tuple(a[r] * hs[r] + g[r] * u for r in range(order))
            u_buf[tile, where] = combine([direct * u] + list(hs))
            return hs

        hs = lax.fori_loop(
            0, span, body, tuple(jnp.zeros((SUB, LANES), F32) for _ in range(order)), unroll=UNROLL)
        for r in range(order):
            run = hs[r]
            for shift in (1, 2, 4):
                factor = jnp.exp(-d_buf[r:r + 1, lanes] * float(span * shift))
                joined = (sub_id >= shift) & ((sub_id < cut) | (sub_id - shift >= cut))
                run = run + jnp.where(joined, factor * pltpu.roll(run, shift, 0), 0.0)
            joined = (sub_id >= 1) & (sub_id != cut)
            before[r, :, lanes] = jnp.where(joined, pltpu.roll(run, 1, 0), 0.0)
            last[r:r + 1, lanes] = run[SUB - 1:SUB]
            tail[r:r + 1, lanes] = jnp.sum(jnp.where(sub_id == cut - 1, run, 0.0), axis=0, keepdims=True)

    for tile in range(tiles):
        scan(tile)

    def decay_over(parts):
        return jnp.exp(-d_buf[...] * (parts * sub).astype(F32))

    states[row] = decay_over(nz - 1 - z) * last[...] + tail[...]

    def state_copy(src, target):
        return remote(
            states.at[src], states.at[src], state_out.at[target], state_in.at[src], {"seq": target})

    def send_state(target, _):
        state_copy(row, target).start()
        return 0

    lax.fori_loop(row + 1, nseq, send_state, 0)
    join_last = remote(last, pair_last, join_out.at[0], join_in.at[0], partner)
    join_carry = remote(carries.at[0], carries.at[1], join_out.at[1], join_in.at[1], partner)
    join_last.start()
    for tile in range(tiles):
        lanes = pl.ds(tile * LANES, LANES)
        for r in range(order):
            power[r, :, lanes] = jnp.exp(-d_buf[r:r + 1, lanes] * away)
    block_decay = jnp.exp(-d_buf[...] * float(rows))

    def add_state(src, carry):
        state_copy(src, row).wait_recv()
        return block_decay * carry + states[src]

    carries[0] = lax.fori_loop(0, row, add_state, jnp.zeros((order, wide), F32))
    join_carry.start()
    to_middle = decay_over(jnp.where(low_chip, z + 1, z - group + 1))
    to_end = jnp.exp(-d_buf[...] * float(group * sub))
    join_last.wait_recv()
    join_carry.wait_recv()

    def swapped(value):
        return jnp.concatenate([value[:, width:], value[:, :width]], axis=1)

    theirs = swapped(pair_last[...])
    carry = carries[0] + swapped(carries[1])
    middle = to_middle * carry + jnp.where(low_chip, last[...], theirs)
    carries[2] = jnp.where(low_chip, carry, middle)
    carries[3] = to_end * middle + theirs

    def finish(tile):
        lanes = pl.ds(tile * LANES, LANES)
        a = [jnp.broadcast_to(jnp.exp(-d_buf[r:r + 1, lanes]), (SUB, LANES)) for r in range(order)]
        hs = tuple(
            before[r, :, lanes] + power[r, :, lanes] * jnp.where(
                sub_id >= cut, carries[2, r:r + 1, lanes], carries[3, r:r + 1, lanes])
            for r in range(order))

        def body(i, hs):
            where = pl.ds(i, SUB, stride=span)
            hs = tuple(a[r] * hs[r] for r in range(order))
            u_buf[tile, where] = combine([u_buf[tile, where]] + list(hs))
            return hs

        lax.fori_loop(0, span, body, hs, unroll=UNROLL)

    def conv_copy(ab, c):
        return remote(conv.at[c, ab], conv.at[c, ab], conv_out.at[ab], conv_in.at[ab], twin)

    per_ab = width // LANES
    for ab in range(2):
        for tile in range(per_ab):
            finish(ab * per_ab + tile)
            conv[core, ab, :, pl.ds(tile * LANES, LANES)] = u_buf[ab * per_ab + tile].astype(BF16)
        conv_copy(ab, core).start()

    def part_terms(delta, c):
        block = lax.rem(z - delta + nz, nz)
        share = 2 * block + c
        return jnp.dot(
            conv[c, 0], wo_a[block, pl.ds(c * width, width)], preferred_element_type=F32) + jnp.dot(
            conv[c, 1], wo_b[share // ny, lax.rem(share, ny)], preferred_element_type=F32)

    for block in range(nz):
        wo_load(block).wait()
        wo_copy(block).wait_recv()
    for copy in lines(1, 1):
        copy.wait_recv()
    for ab in range(2):
        conv_copy(ab, 1 - core).wait_recv()

    def target_of(side, r, i):
        length = (up, down)[side][r]
        h = length - i + 1
        return (way[side] * h) % nz, slot_of(side, r, h)

    def sum_copy(side, r, i):
        n = index[side][(r, i)]
        delta, k = target_of(side, r, i)
        src = arrived.at[side, index[side][(r, i - 1)]] if k is None else leaving.at[side, n]
        return remote(src, arrived.at[side, n], sum_out.at[side, n], sum_in.at[side, n], ring_dev[1 - side])

    have = set()

    def need(delta):
        if delta not in have:
            have.add(delta)
            part[delta] = part_terms(delta, 0) + part_terms(delta, 1)

    def finish_sum(r):
        total = None
        if (-r) % nz < group:
            need(0)
            total = part[0, own_rows_of_slot(own_slot(r))]
        for side in (0, 1):
            length = (up, down)[side][r]
            if length > 0:
                sum_copy(side, r, length).wait_recv()
                got = arrived[side, index[side][(r, length)]].astype(F32)
                total = got if total is None else total + got
        out[own_rows(r)] = total.astype(BF16)

    def own_rows_of_slot(k):
        return slot_rows(k)

    ends = {r: max([index[s][(r, (up, down)[s][r])] for s in (0, 1) if (up, down)[s][r] > 0] + [0]) + LAG for r in range(nz)}
    for step in range(count + LAG + 1):
        for side in (0, 1):
            if step < count:
                r, i = lists[side][step]
                delta, k = target_of(side, r, i)
                if k is not None:
                    need(delta)
                if i > 1:
                    sum_copy(side, r, i - 1).wait_recv()
                if k is not None:
                    value = part[delta, slot_rows(k)]
                    if i > 1:
                        value = value + arrived[side, index[side][(r, i - 1)]].astype(F32)
                    leaving[side, index[side][(r, i)]] = value.astype(BF16)
                sum_copy(side, r, i).start()
        for r in range(nz):
            if ends[r] == step:
                finish_sum(r)

    for side in (0, 1):
        for item in lists[side]:
            ring_copy(side, *item).wait_send()
            sum_copy(side, *item).wait_send()
            if slot_of(side, *item) is not None:
                pair_copy(side, *item).wait_send()
    for n in range(group):
        own_pair(n).wait_send()
    far_wi.wait_send()

    @pl.when(core == lax.rem(row, 2))
    def _():
        for c in range(2):
            far_wo(c).wait_send()

    for which in range(2):
        for stage in range(2):
            for copy in lines(which, stage):
                copy.wait_send()
    for copy in params:
        copy.wait_send()
    for block in range(nz):
        wo_copy(block).wait_send()
    join_last.wait_send()
    join_carry.wait_send()
    for ab in range(2):
        conv_copy(ab, core).wait_send()

    def drain_state(target, _):
        state_copy(row, target).wait_send()
        return 0

    lax.fori_loop(row + 1, nseq, drain_state, 0)


def per_device(nseq, nchan, tokens, w_in, residues, decays, skip_gain, w_out):
    rows, width = tokens.shape
    order = residues.shape[1]
    nz = nchan // 2
    ny = nseq // NX
    group = nz // 2
    mine = rows // 2
    wide = 2 * width
    count = len(paths(nz)[2][0])
    dma = pltpu.SemaphoreType.DMA
    vmem = pl.BlockSpec(memory_space=pltpu.VMEM)
    hbm = pl.BlockSpec(memory_space=pl.ANY)
    flops = 4 * rows * width * nchan * width
    return pl.pallas_call(
        functools.partial(kernel, nseq, nz, rows, width, order),
        out_shape=jax.ShapeDtypeStruct((rows, width), BF16),
        in_specs=[hbm, hbm, vmem, vmem, vmem, hbm],
        out_specs=vmem,
        scratch_shapes=[
            pltpu.VMEM((nchan, mine, width), BF16),
            pltpu.VMEM((2, 1, rows // nz, width), BF16),
            pltpu.VMEM((nchan, width, width), BF16),
            pltpu.VMEM((NX, ny, width, width), BF16),
            pltpu.VMEM((nz, 2 * width, width), BF16),
            pltpu.VMEM((NX, ny, width, width), BF16),
            pltpu.VMEM((mine, wide), F32),
            pltpu.VMEM((wide // LANES, mine, LANES), F32),
            pltpu.VMEM((2, 2, mine, width), BF16),
            pltpu.VMEM((nz, mine, width), F32),
            pltpu.VMEM((2, count, rows // nz, width), BF16),
            pltpu.VMEM((2, count, rows // nz, width), BF16),
            pltpu.VMEM((order, width), F32),
            pltpu.VMEM((order, width), F32),
            pltpu.VMEM((1, width), F32),
            pltpu.VMEM((order, wide), F32),
            pltpu.VMEM((order, wide), F32),
            pltpu.VMEM((1, wide), F32),
            pltpu.VMEM((order, SUB, wide), F32),
            pltpu.VMEM((order, SUB, wide), F32),
            pltpu.VMEM((order, wide), F32),
            pltpu.VMEM((order, wide), F32),
            pltpu.VMEM((nseq, order, wide), F32),
            pltpu.VMEM((4, order, wide), F32),
            pltpu.VMEM((order, wide), F32),
            dma((2, count)), dma((2, count)),
            dma((2, count)), dma((2, count)),
            dma((group,)), dma((group,)),
            dma((2, count)), dma((2, count)),
            dma((nseq,)), dma((nseq,)),
            dma((2,)), dma((2,)),
            dma((nz,)), dma((nz,)),
            dma((2,)), dma((3,)),
            dma((NX + ny - 2, 2, 2)), dma((NX + ny - 2, 2, 2)),
            dma((3,)), dma((3,)),
            dma((2,)), dma((2,)),
            dma((group + 1 + nz,)),
        ],
        compiler_params=pltpu.CompilerParams(
            collective_id=0, has_side_effects=True, vmem_limit_bytes=60 * 1024 * 1024),
        cost_estimate=pl.CostEstimate(flops=flops, bytes_accessed=6 * 1024 * 1024, transcendentals=0),
    )(tokens, w_in.reshape(nchan, width, width), residues.T, decays.T, skip_gain.reshape(1, width), w_out)


def solution(mesh):
    in_specs = (
        P("seq", "chan"),
        P(None, "chan"),
        P("chan", None),
        P("chan", None),
        P("chan"),
        P("chan", None),
    )
    return jax.shard_map(
        functools.partial(per_device, mesh.shape["seq"], mesh.shape["chan"]),
        mesh=mesh, in_specs=in_specs, out_specs=P("seq", "chan"), check_vma=False)
```

```python
import functools

import jax
import jax.numpy as jnp
from jax import lax
from jax.experimental import pallas as pl
from jax.experimental.pallas import tpu as pltpu
from jax.sharding import PartitionSpec as P

MESH = pl.DeviceIdType.MESH
F32 = jnp.float32
BF16 = jnp.bfloat16
SUB = 8
LANES = 128
UNROLL = 8
LAG = 4
SUM_LAG = 4
NX = 4
WI_FIRST, WI_SECOND, WI_RELAY, WI_DONE = 3, 5, 8, 13
WO_START, WO_FIRST, WO_SECOND, WO_RELAY = 5, 9, 12, 17


def hop_counts(nz):
    group = nz // 2
    up, down = {}, {}
    for r in range(nz):
        last = r + group - 1
        if r == 0:
            up[r], down[r] = last, 0
        elif last >= nz:
            up[r], down[r] = last - nz, nz - r
        elif last < nz - r:
            up[r], down[r] = last, 0
        else:
            up[r], down[r] = 0, nz - r
    return up, down


def schedule(lengths, lag):
    left = {r: n for r, n in lengths.items() if n > 0}
    ready = {r: 0 for r in left}
    items, place = [], 0
    while left:
        able = [r for r in left if ready[r] <= place]
        if able:
            r = max(able, key=lambda r: (left[r], -r))
            items.append((r, lengths[r] - left[r] + 1))
            left[r] -= 1
            ready[r] = place + lag
            if left[r] == 0:
                del left[r]
        place += 1
    return items


def paths(nz, lag):
    up, down = hop_counts(nz)
    first = schedule(up, lag)
    mirror = {r: (nz // 2 + 1 - r) % nz for r in range(nz)}
    second = [(mirror[r], h) for r, h in first]
    assert sorted(second) == sorted((r, h) for r in down for h in range(1, down[r] + 1))
    return up, down, (first, second)


def kernel(
    nseq, nz, rows, width, order,
    tokens, w_in, residues_in, decays_in, skip_in, w_out, out,
    x_buf, relay, result, wi_a, wi_b, wo_a, wo_b, acc, u_buf, conv, part, arrived, leaving,
    residues, decays, skip, far_res, far_dec, far_skip, g_buf, d_buf, k_buf, power, before, slot_end, slot_start, last, states, carries, pair_last,
    ring_in, ring_out, pair_in, pair_out, own_in, own_out, sum_in, sum_out, state_in, state_out, conv_in, conv_out,
    wo_in, wo_sent, far_in, far_out, line_in, line_out, pass_in, pass_out, prm_in, prm_out, join_in, join_out, local, own_prm, out_sem,
):
    row = lax.axis_index("seq")
    chan = lax.axis_index("chan")
    z, core = chan // 2, chan % 2
    ny = nseq // NX
    x, y = row // ny, row % ny
    group = nz // 2
    sub = rows // nz
    mine = group * sub
    half = mine // 2
    span = half // SUB
    slot_order = (1, 2, 0, 3) if group == 4 else tuple(range(group))
    per_half = group // 2
    seg = SUB // per_half
    up, down, lists = paths(nz, LAG)
    sum_lists = paths(nz, SUM_LAG)[2]
    count = len(lists[0])
    index = [{item: n for n, item in enumerate(items)} for items in lists]
    sum_index = [{item: n for n, item in enumerate(items)} for items in sum_lists]
    way = (1, -1)

    def at(dz, c):
        return {"chan": 2 * lax.rem(z + dz + nz, nz) + c}

    low_chip = z < group
    near = jnp.where(low_chip, 0, 1)

    ring_dev = [at(1, core), at(nz - 1, core)]
    twin = at(0, 1 - core)
    partner = at(group, core)
    across = at(group, 1 - core)

    barrier = pltpu.get_barrier_semaphore()
    for other in (ring_dev[0], ring_dev[1], twin, partner, across):
        pl.semaphore_signal(barrier, inc=1, device_id=other, device_id_type=MESH)

    def greet(step, _):
        pl.semaphore_signal(
            barrier, inc=1, device_id={"seq": lax.rem(row + step, nseq)}, device_id_type=MESH)
        return 0

    lax.fori_loop(1, nseq, greet, 0)

    def remote(src, dst, send, recv, device):
        return pltpu.make_async_remote_copy(
            src_ref=src, dst_ref=dst, send_sem=send, recv_sem=recv, device_id=device, device_id_type=MESH)

    def slot_of(side, r, h):
        j = (way[side] * h - r) % nz
        return slot_order.index(group - 1 - j) if j < group else None

    def source_block(side, h, c):
        return 2 * lax.rem(z - way[side] * h + 2 * nz, nz) + c

    def slot_rows(k):
        return pl.ds(k * sub, sub)

    relays = [[item for item in lists[side] if slot_of(side, *item) is None] for side in (0, 1)]

    def place_of(side, r, h, block):
        k = slot_of(side, r, h)
        if k is None:
            return relay.at[side, relays[side].index((r, h))]
        return x_buf.at[block, slot_rows(k)]

    def own_rows(r):
        q = lax.rem(z + r, nz)
        return pl.ds(pl.multiple_of(q * sub, sub), sub)

    def ring_copy(side, r, h):
        block = source_block(side, h - 1, core)
        src = tokens.at[own_rows(r)] if h == 1 else place_of(side, r, h - 1, block)
        n = index[side][(r, h)]
        return remote(src, place_of(side, r, h, block), ring_out.at[side, n], ring_in.at[side, n], ring_dev[side])

    def pair_copy(side, r, h, from_twin=False):
        block = source_block(side, h, 1 - core if from_twin else core)
        ref = place_of(side, r, h, block)
        n = index[side][(r, h)]
        return remote(ref, ref, pair_out.at[side, n], pair_in.at[side, n], twin)

    own_parts = [r for r in range(nz) if (-r) % nz < group]

    def own_slot(r):
        return slot_order.index(group - 1 - (-r) % nz)

    def own_load(n):
        r = own_parts[n]
        return pltpu.make_async_copy(
            tokens.at[own_rows(r)], x_buf.at[chan, slot_rows(own_slot(r))], local.at[n])

    def own_pair(n):
        r = own_parts[n]
        return remote(
            tokens.at[own_rows(r)], x_buf.at[chan, slot_rows(own_slot(r))], own_out.at[n], own_in.at[n], twin)

    wi_load = pltpu.make_async_copy(w_in, wi_a, local.at[group])

    far_wi = remote(w_in.at[row], wi_b.at[x, y], far_out.at[0], far_in.at[0], partner)

    def far_wo(c):
        cols = pl.ds(pl.multiple_of((2 * (row // 2) + c) * width, LANES), width)
        device = {"chan": 2 * lax.rem(z + group, nz) + c}
        return remote(w_out.at[:, cols], wo_b.at[x, y], far_out.at[1 + c], far_in.at[1], device)

    low_rows, high_rows = pl.ds(0, width // 2), pl.ds(width // 2, width // 2)

    def lines(which):
        buf = (wi_b, wo_b)[which]
        copies = []
        for step in range(1, NX):
            n = (step - 1, which)
            device = {"seq": lax.rem(x + step, NX) * ny + y}
            ref = buf.at[x, y, low_rows]
            copies.append(remote(ref, ref, line_out.at[n], line_in.at[n], device))
        for step in range(1, ny):
            n = (NX - 1 + step - 1, which)
            device = {"seq": x * ny + lax.rem(y + step, ny)}
            ref = buf.at[x, y, high_rows]
            copies.append(remote(ref, ref, line_out.at[n], line_in.at[n], device))
        return copies

    def pass_on(which, axis, i):
        n, p = ((NX, x), (ny, y))[axis]
        p = lax.rem(p + n + (0, 0, 0, 0, -1, 1)[i], n)
        part_i, step = (0, 1, 1, 0, 0, 1)[i], (1, 1, -1, -1, 1, -1)[i]
        buf = (wi_b, wo_b)[which]
        if axis == 0:
            ref = buf.at[p, pl.ds(part_i * (ny // 2), ny // 2), high_rows]
            device = {"seq": lax.rem(x + step + NX, NX) * ny + y}
        else:
            ref = buf.at[pl.ds(part_i * (NX // 2), NX // 2), p, low_rows]
            device = {"seq": x * ny + lax.rem(y + step + ny, ny)}
        return remote(ref, ref, pass_out.at[which, axis, i], pass_in.at[which, axis, i], device)

    def pass_list(which, name):
        picks = {"own": (0, 2, 1, 3), "first": (0, 2), "on": (4, 5), "rest": (1, 3, 4, 5)}[name]
        short = {"own": (0, 1), "first": (), "on": (), "rest": (0, 1)}[name]
        return [
            pass_on(which, axis, i)
            for place in range(4) for axis in (0, 1)
            for i in ((picks if (NX, ny)[axis] == 4 else short)[place:place + 1])]

    params = [
        remote(src, dst, prm_out.at[n], prm_in.at[n], partner)
        for n, (src, dst) in enumerate(((residues_in, far_res), (decays_in, far_dec), (skip_in, far_skip)))]
    own_params = [
        pltpu.make_async_copy(src, dst, own_prm.at[n])
        for n, (src, dst) in enumerate(((residues_in, residues), (decays_in, decays), (skip_in, skip)))]

    def wo_cols(block, c):
        return pl.ds(pl.multiple_of((2 * block + c) * width, LANES), width)

    def wo_copy(block):
        return remote(
            w_out.at[:, wo_cols(block, 1 - core)], wo_a.at[block, pl.ds(core * width, width)],
            wo_sent.at[block], wo_in.at[block], twin)

    def wo_load(block):
        return pltpu.make_async_copy(
            w_out.at[:, wo_cols(block, core)], wo_a.at[block, pl.ds(core * width, width)],
            local.at[group + 1 + block])

    def half_rows(hf):
        return pl.ds(hf * half, half)

    def project(delta, hf, ab, first):
        total = None
        source = lax.rem(z - delta + nz, nz)
        for c in range(2):
            block = 2 * source + c
            weights = wi_a[block] if ab == 0 else wi_b[block // ny, lax.rem(block, ny)]
            term = jnp.dot(x_buf[block, half_rows(hf)], weights, preferred_element_type=F32)
            total = term if total is None else total + term
        if first:
            acc[ab, half_rows(hf)] = total
        else:
            acc[ab, half_rows(hf)] += total

    cut = jnp.where(low_chip, group - 1 - z, 0)
    sub_id = lax.broadcasted_iota(jnp.int32, (SUB, LANES), 0)
    in_slot = sub_id % seg
    tiles = width // LANES

    def combine(terms):
        while len(terms) > 1:
            terms = [terms[k] + terms[k + 1] if k + 1 < len(terms) else terms[k] for k in range(0, len(terms), 2)]
        return terms[0]

    def scan(turn, tile, hf):
        lanes = pl.ds(tile * LANES, LANES)
        spot = turn * tiles + tile
        ab = jnp.where(low_chip, turn, 1 - turn)
        u_buf[spot, half_rows(hf)] = acc[ab, half_rows(hf), lanes].astype(BF16).astype(F32)
        a = [jnp.broadcast_to(jnp.exp(-d_buf[turn, r:r + 1, lanes]), (SUB, LANES)) for r in range(order)]
        g = [jnp.broadcast_to(g_buf[turn, r:r + 1, lanes], (SUB, LANES)) for r in range(order)]
        direct = jnp.broadcast_to(k_buf[turn, :, lanes], (SUB, LANES))

        def body(i, hs):
            where = pl.ds(hf * half + i, SUB, stride=span)
            u = u_buf[spot, where]
            hs = tuple(a[r] * hs[r] + g[r] * u for r in range(order))
            u_buf[spot, where] = combine([direct * u] + list(hs))
            return hs

        hs = lax.fori_loop(
            0, span, body, tuple(jnp.zeros((SUB, LANES), F32) for _ in range(order)), unroll=UNROLL)
        for r in range(order):
            run = hs[r]
            for shift in (1, 2, 4):
                if shift < seg:
                    factor = jnp.exp(-d_buf[turn, r:r + 1, lanes] * float(span * shift))
                    run = run + jnp.where(in_slot >= shift, factor * pltpu.roll(run, shift, 0), 0.0)
            before[turn, hf, r, :, lanes] = jnp.where(in_slot >= 1, pltpu.roll(run, 1, 0), 0.0)
            for n in range(per_half):
                k = slot_order[hf * per_half + n]
                slot_end[turn, k, r:r + 1, lanes] = run[(n + 1) * seg - 1:(n + 1) * seg]

    early = [(turn, tile) for turn in range(2) for tile in range(tiles)]

    for n in range(group):
        own_load(n).start()
    wi_load.start()
    for copy in own_params:
        copy.start()
    pl.semaphore_wait(barrier, nseq + 4)
    far_wi.start()
    for side in (0, 1):
        ring_copy(side, *lists[side][0]).start()
    for copy in params:
        copy.start()
    for n in range(group):
        own_pair(n).start()

    sources = {}
    for side in (0, 1):
        for n, (r, h) in enumerate(lists[side]):
            if slot_of(side, r, h) is not None:
                sources.setdefault(((way[side] * h) % nz, slot_of(side, r, h) // per_half), []).append((side, r, h, n))
    whole = {key: max(n for _, _, _, n in got) + LAG + 1 for key, got in sources.items()}

    arrived_items, fresh = set(), []

    def arrive(side, r, h):
        if (side, r, h) not in arrived_items:
            arrived_items.add((side, r, h))
            fresh.append((side, r, h))
            ring_copy(side, r, h).wait_recv()

    def hook(place):
        if place == WO_START:
            @pl.when(core == lax.rem(row, 2))
            def _():
                for c in range(2):
                    far_wo(c).start()
        if place == WO_FIRST:
            far_wo(0).wait_recv()
            for copy in lines(1):
                copy.start()
        if place == WO_SECOND:
            for copy in lines(1):
                copy.wait_recv()
            for copy in pass_list(1, "own"):
                copy.start()
        if place == WO_RELAY:
            for copy in pass_list(1, "first"):
                copy.wait_recv()
            for copy in pass_list(1, "on"):
                copy.start()

    far_ready = False
    projected = []
    for step in range(max(count + LAG + 2, WI_DONE + 1)):
        for side in (0, 1):
            if 0 < step < count:
                r, h = lists[side][step]
                if h > 1:
                    arrive(side, r, h - 1)
                ring_copy(side, r, h).start()
        for side in (0, 1):
            if LAG <= step < count + LAG:
                arrive(side, *lists[side][step - LAG])
            for item in list(fresh):
                fresh.remove(item)
                if slot_of(*item) is not None:
                    pair_copy(*item).start()
        if step == 1:
            for block in range(nz):
                wo_load(block).start()
                wo_copy(block).start()
        if step == 2:
            for n in range(group):
                own_load(n).wait()
                own_pair(n).wait_recv()
            wi_load.wait()
            for hf in range(2):
                project(0, hf, 0, True)
                projected.append((0, hf))
        hook(step)
        if step == WI_FIRST:
            far_wi.wait_recv()
            for copy in lines(0):
                copy.start()
        if step == WI_SECOND:
            for copy in lines(0):
                copy.wait_recv()
            for copy in pass_list(0, "own"):
                copy.start()
        if step == WI_RELAY:
            for copy in pass_list(0, "first"):
                copy.wait_recv()
            for copy in pass_list(0, "on"):
                copy.start()
        if step == WI_DONE:
            for copy in pass_list(0, "rest"):
                copy.wait_recv()
            far_ready = True
            for delta, hf in projected:
                project(delta, hf, 1, delta == 0)
            for copy in params:
                copy.wait_recv()
            for copy in own_params:
                copy.wait()
            g_buf[near] = residues[...] * jnp.sqrt(decays[...])
            g_buf[1 - near] = far_res[...] * jnp.sqrt(far_dec[...])
            d_buf[near] = decays[...]
            d_buf[1 - near] = far_dec[...]
            k_buf[near] = skip[...]
            k_buf[1 - near] = far_skip[...]
        for key, ready in whole.items():
            if ready == step:
                for side, r, h, _ in sources[key]:
                    pair_copy(side, r, h, True).wait_recv()
                project(*key, 0, False)
                if far_ready:
                    project(*key, 1, False)
                projected.append(key)
        if far_ready and len([1 for _, hf in projected if hf == 0]) == nz and early:
            scan(*early.pop(0), 0)
    assert far_ready and len(projected) == 2 * nz
    for turn, tile in early:
        scan(turn, tile, 0)

    def decay_over(turn, parts):
        return jnp.exp(-d_buf[turn] * (parts * sub).astype(F32))

    def state_copy(turn, src, target):
        return remote(
            states.at[turn, src], states.at[turn, src], state_out.at[turn, target], state_in.at[turn, src],
            {"seq": target})

    def join_last(turn):
        return remote(last.at[turn], pair_last.at[turn], join_out.at[turn, 0], join_in.at[turn, 0], partner)

    def join_carry(turn):
        return remote(
            carries.at[turn, 0], carries.at[turn, 1], join_out.at[turn, 1], join_in.at[turn, 1], partner)

    for turn in range(2):
        hook(100 + turn)
        for tile in range(tiles):
            scan(turn, tile, 1)
        slot_decay = jnp.exp(-d_buf[turn] * float(sub))
        run = tail = jnp.zeros((order, width), F32)
        for k in range(group):
            run = jnp.where(cut == k, 0.0, run * slot_decay) + slot_end[turn, k]
            tail = jnp.where(cut == k + 1, run, tail)
        last[turn] = run
        states[turn, row] = decay_over(turn, nz - 1 - z) * run + tail

        def send_state(target, _, turn=turn):
            state_copy(turn, row, target).start()
            return 0

        lax.fori_loop(row + 1, nseq, send_state, 0)
        join_last(turn).start()

    def get_carry(turn):
        block_decay = jnp.exp(-d_buf[turn] * float(rows))

        def add_state(src, carry):
            state_copy(turn, src, row).wait_recv()
            return block_decay * carry + states[turn, src]

        carries[turn, 0] = lax.fori_loop(0, row, add_state, jnp.zeros((order, width), F32))
        join_carry(turn).start()

    def set_powers(turn):
        for tile in range(tiles):
            lanes = pl.ds(tile * LANES, LANES)
            for r in range(order):
                power[turn, r, :, lanes] = jnp.exp(
                    -d_buf[turn, r:r + 1, lanes] * (in_slot.astype(F32) * float(span)))

    def join(turn):
        to_middle = decay_over(turn, jnp.where(low_chip, z + 1, z - group + 1))
        to_end = jnp.exp(-d_buf[turn] * float(group * sub))
        join_last(turn).wait_recv()
        join_carry(turn).wait_recv()
        carry = carries[turn, 0] + carries[turn, 1]
        middle = to_middle * carry + jnp.where(low_chip, last[turn], pair_last[turn])
        begin = jnp.where(low_chip, carry, middle)
        slot_decay = jnp.exp(-d_buf[turn] * float(sub))
        ahead = jnp.where(cut > 0, to_end * middle + pair_last[turn], begin)
        for k in range(group):
            if k > 0:
                ahead = jnp.where(cut == k, begin, ahead * slot_decay + slot_end[turn, k - 1])
            slot_start[turn, k] = ahead

    def finish(turn, tile, hf):
        lanes = pl.ds(tile * LANES, LANES)
        spot = turn * tiles + tile
        a = [jnp.broadcast_to(jnp.exp(-d_buf[turn, r:r + 1, lanes]), (SUB, LANES)) for r in range(order)]
        hs = []
        for r in range(order):
            start = None
            for n in range(per_half):
                value = slot_start[turn, slot_order[hf * per_half + n], r:r + 1, lanes]
                start = value if start is None else jnp.where(sub_id >= n * seg, value, start)
            hs.append(before[turn, hf, r, :, lanes] + power[turn, r, :, lanes] * start)

        def body(i, hs):
            where = pl.ds(hf * half + i, SUB, stride=span)
            hs = tuple(a[r] * hs[r] for r in range(order))
            u_buf[spot, where] = combine([u_buf[spot, where]] + list(hs))
            return hs

        lax.fori_loop(0, span, body, tuple(hs), unroll=UNROLL)
        conv[core, turn, half_rows(hf), lanes] = u_buf[spot, half_rows(hf)].astype(BF16)

    def conv_copy(turn, hf, c):
        ref = conv.at[c, turn, half_rows(hf)]
        return remote(ref, ref, conv_out.at[turn, hf], conv_in.at[turn, hf], twin)

    for turn in range(2):
        hook(102 + turn)
        set_powers(turn)
    for turn in range(2):
        get_carry(turn)
        hook(104 + turn)
    for turn in range(2):
        join(turn)
        for hf in (1, 0):
            for tile in range(tiles):
                finish(turn, tile, hf)
            conv_copy(turn, hf, core).start()

    def part_terms(delta, hf, c):
        block = lax.rem(z - delta + nz, nz)
        share = 2 * block + c
        return jnp.dot(
            conv[c, near, half_rows(hf)], wo_a[block, pl.ds(c * width, width)], preferred_element_type=F32) + jnp.dot(
            conv[c, 1 - near, half_rows(hf)], wo_b[share // ny, lax.rem(share, ny)], preferred_element_type=F32)

    for block in range(nz):
        wo_load(block).wait()
        wo_copy(block).wait_recv()
    for copy in pass_list(1, "rest"):
        copy.wait_recv()

    def target_of(side, r, i):
        length = (up, down)[side][r]
        h = length - i + 1
        return (way[side] * h) % nz, slot_of(side, r, h)

    def sum_copy(side, r, i):
        n = sum_index[side][(r, i)]
        delta, k = target_of(side, r, i)
        src = arrived.at[side, sum_index[side][(r, i - 1)]] if k is None else leaving.at[side, n]
        return remote(src, arrived.at[side, n], sum_out.at[side, n], sum_in.at[side, n], ring_dev[1 - side])

    have, seen = set(), set()

    def need(delta, k):
        hf = k // per_half
        if hf not in seen:
            seen.add(hf)
            for turn in range(2):
                conv_copy(turn, hf, 1 - core).wait_recv()
        if (delta, hf) not in have:
            have.add((delta, hf))
            part[delta, half_rows(hf)] = part_terms(delta, hf, 0) + part_terms(delta, hf, 1)

    def out_copy(r):
        return pltpu.make_async_copy(result.at[r], out.at[own_rows(r)], out_sem.at[r])

    def finish_sum(r):
        total = None
        if (-r) % nz < group:
            need(0, own_slot(r))
            total = part[0, slot_rows(own_slot(r))]
        for side in (0, 1):
            length = (up, down)[side][r]
            if length > 0:
                sum_copy(side, r, length).wait_recv()
                got = arrived[side, sum_index[side][(r, length)]].astype(F32)
                total = got if total is None else total + got
        result[r] = total.astype(BF16)
        out_copy(r).start()

    drains = []
    for side in (0, 1):
        for item in lists[side]:
            drains.append(ring_copy(side, *item).wait_send)
            if slot_of(side, *item) is not None:
                drains.append(pair_copy(side, *item).wait_send)
    drains += [own_pair(n).wait_send for n in range(group)] + [far_wi.wait_send]
    for which in range(2):
        drains += [copy.wait_send for copy in lines(which) + pass_list(which, "own") + pass_list(which, "on")]
    drains += [copy.wait_send for copy in params]
    drains += [wo_copy(block).wait_send for block in range(nz)]
    for turn in range(2):
        drains += [join_last(turn).wait_send, join_carry(turn).wait_send]
        drains += [conv_copy(turn, hf, core).wait_send for hf in range(2)]

    def drain_far():
        @pl.when(core == lax.rem(row, 2))
        def _():
            for c in range(2):
                far_wo(c).wait_send()

    def drain_states():
        def one(target, _):
            for turn in range(2):
                state_copy(turn, row, target).wait_send()
            return 0

        lax.fori_loop(row + 1, nseq, one, 0)

    drains += [drain_far, drain_states]
    batch = -(-len(drains) // (count - 2))

    ends = {r: max([sum_index[s][(r, (up, down)[s][r])] for s in (0, 1) if (up, down)[s][r] > 0] + [0]) + SUM_LAG for r in range(nz)}
    for step in range(count + SUM_LAG + 1):
        for side in (0, 1):
            if step < count:
                r, i = sum_lists[side][step]
                delta, k = target_of(side, r, i)
                if k is not None:
                    need(delta, k)
                if i > 1:
                    sum_copy(side, r, i - 1).wait_recv()
                if k is not None:
                    value = part[delta, slot_rows(k)]
                    if i > 1:
                        value = value + arrived[side, sum_index[side][(r, i - 1)]].astype(F32)
                    leaving[side, sum_index[side][(r, i)]] = value.astype(BF16)
                sum_copy(side, r, i).start()
        if step > 0:
            for wait in drains[:batch]:
                wait()
            del drains[:batch]
        for r in range(nz):
            if ends[r] == step:
                finish_sum(r)

    for side in (0, 1):
        for item in sum_lists[side]:
            sum_copy(side, *item).wait_send()
    for r in range(nz):
        out_copy(r).wait()
    assert not drains


def per_device(nseq, nchan, tokens, w_in, residues, decays, skip_gain, w_out):
    rows, width = tokens.shape
    order = residues.shape[1]
    nz = nchan // 2
    ny = nseq // NX
    group = nz // 2
    mine = rows // 2
    count = len(paths(nz, LAG)[2][0])
    dma = pltpu.SemaphoreType.DMA
    hbm = pl.BlockSpec(memory_space=pl.ANY)
    flops = 4 * rows * width * nchan * width
    return pl.pallas_call(
        functools.partial(kernel, nseq, nz, rows, width, order),
        out_shape=jax.ShapeDtypeStruct((rows, width), BF16),
        in_specs=[hbm] * 6,
        out_specs=hbm,
        scratch_shapes=[
            pltpu.VMEM((nchan, mine, width), BF16),
            pltpu.VMEM((2, 1, rows // nz, width), BF16),
            pltpu.VMEM((nz, rows // nz, width), BF16),
            pltpu.VMEM((nchan, width, width), BF16),
            pltpu.VMEM((NX, ny, width, width), BF16),
            pltpu.VMEM((nz, 2 * width, width), BF16),
            pltpu.VMEM((NX, ny, width, width), BF16),
            pltpu.VMEM((2, mine, width), F32),
            pltpu.VMEM((2 * width // LANES, mine, LANES), F32),
            pltpu.VMEM((2, 2, mine, width), BF16),
            pltpu.VMEM((nz, mine, width), F32),
            pltpu.VMEM((2, count, rows // nz, width), BF16),
            pltpu.VMEM((2, count, rows // nz, width), BF16),
            pltpu.VMEM((order, width), F32),
            pltpu.VMEM((order, width), F32),
            pltpu.VMEM((1, width), F32),
            pltpu.VMEM((order, width), F32),
            pltpu.VMEM((order, width), F32),
            pltpu.VMEM((1, width), F32),
            pltpu.VMEM((2, order, width), F32),
            pltpu.VMEM((2, order, width), F32),
            pltpu.VMEM((2, 1, width), F32),
            pltpu.VMEM((2, order, SUB, width), F32),
            pltpu.VMEM((2, 2, order, SUB, width), F32),
            pltpu.VMEM((2, group, order, width), F32),
            pltpu.VMEM((2, group, order, width), F32),
            pltpu.VMEM((2, order, width), F32),
            pltpu.VMEM((2, nseq, order, width), F32),
            pltpu.VMEM((2, 2, order, width), F32),
            pltpu.VMEM((2, order, width), F32),
            dma((2, count)), dma((2, count)),
            dma((2, count)), dma((2, count)),
            dma((group,)), dma((group,)),
            dma((2, count)), dma((2, count)),
            dma((2, nseq)), dma((2, nseq)),
            dma((2, 2)), dma((2, 2)),
            dma((nz,)), dma((nz,)),
            dma((2,)), dma((3,)),
            dma((NX + ny - 2, 2)), dma((NX + ny - 2, 2)),
            dma((2, 2, 6)), dma((2, 2, 6)),
            dma((3,)), dma((3,)),
            dma((2, 2)), dma((2, 2)),
            dma((group + 1 + nz,)),
            dma((3,)),
            dma((nz,)),
        ],
        compiler_params=pltpu.CompilerParams(
            collective_id=0, has_side_effects=True, vmem_limit_bytes=56 * 1024 * 1024),
        cost_estimate=pl.CostEstimate(flops=flops, bytes_accessed=6 * 1024 * 1024, transcendentals=0),
    )(tokens, w_in.reshape(nchan, width, width), residues.T, decays.T, skip_gain.reshape(1, width), w_out)


def solution(mesh):
    in_specs = (
        P("seq", "chan"),
        P(None, "chan"),
        P("chan", None),
        P("chan", None),
        P("chan"),
        P("chan", None),
    )
    return jax.shard_map(
        functools.partial(per_device, mesh.shape["seq"], mesh.shape["chan"]),
        mesh=mesh, in_specs=in_specs, out_specs=P("seq", "chan"), check_vma=False)
```

```python
import functools

import jax
import jax.numpy as jnp
from jax import lax
from jax.experimental import pallas as pl
from jax.experimental.pallas import tpu as pltpu
from jax.sharding import PartitionSpec as P

MESH = pl.DeviceIdType.MESH
F32 = jnp.float32
BF16 = jnp.bfloat16
SUB = 8
LANES = 128
UNROLL = 16
LAG = 4
SUM_LAG = 6
NX = 4
WI_FIRST, WI_SECOND, WI_RELAY, WI_DONE = 3, 5, 8, 13
WO_START, WO_FIRST, WO_SECOND, WO_RELAY = 5, 9, 12, 17


def hop_counts(nz):
    group = nz // 2
    up, down = {}, {}
    for r in range(nz):
        last = r + group - 1
        if r == 0:
            up[r], down[r] = last, 0
        elif last >= nz:
            up[r], down[r] = last - nz, nz - r
        elif last < nz - r:
            up[r], down[r] = last, 0
        else:
            up[r], down[r] = 0, nz - r
    return up, down


def schedule(lengths, lag):
    left = {r: n for r, n in lengths.items() if n > 0}
    ready = {r: 0 for r in left}
    items, place = [], 0
    while left:
        able = [r for r in left if ready[r] <= place]
        if able:
            r = max(able, key=lambda r: (left[r], -r))
            items.append((r, lengths[r] - left[r] + 1))
            left[r] -= 1
            ready[r] = place + lag
            if left[r] == 0:
                del left[r]
        place += 1
    return items


def paths(nz, lag):
    up, down = hop_counts(nz)
    first = schedule(up, lag)
    mirror = {r: (nz // 2 + 1 - r) % nz for r in range(nz)}
    second = [(mirror[r], h) for r, h in first]
    assert sorted(second) == sorted((r, h) for r in down for h in range(1, down[r] + 1))
    return up, down, (first, second)


def kernel(
    nseq, nz, rows, width, order,
    tokens, w_in, residues_in, decays_in, skip_in, w_out, out,
    x_buf, relay, result, wi_a, wi_b, wo_a, wo_b, acc, u_buf, conv, part, arrived, leaving,
    residues, decays, skip, far_res, far_dec, far_skip, g_buf, d_buf, k_buf, power, before, slot_end, slot_start, last, states, carries, pair_last,
    ring_in, ring_out, pair_in, pair_out, own_in, own_out, sum_in, sum_out, state_in, state_out, conv_in, conv_out,
    wo_in, wo_sent, far_in, far_out, line_in, line_out, pass_in, pass_out, prm_in, prm_out, join_in, join_out, local, own_prm, out_sem,
):
    row = lax.axis_index("seq")
    chan = lax.axis_index("chan")
    z, core = chan // 2, chan % 2
    ny = nseq // NX
    x, y = row // ny, row % ny
    group = nz // 2
    sub = rows // nz
    mine = group * sub
    half = mine // 2
    span = half // SUB
    slot_order = (1, 2, 0, 3) if group == 4 else tuple(range(group))
    per_half = group // 2
    seg = SUB // per_half
    up, down, lists = paths(nz, LAG)
    sum_lists = paths(nz, SUM_LAG)[2]
    count = len(lists[0])
    index = [{item: n for n, item in enumerate(items)} for items in lists]
    sum_index = [{item: n for n, item in enumerate(items)} for items in sum_lists]
    way = (1, -1)

    def at(dz, c):
        return {"chan": 2 * lax.rem(z + dz + nz, nz) + c}

    low_chip = z < group
    near = jnp.where(low_chip, 0, 1)

    ring_dev = [at(1, core), at(nz - 1, core)]
    twin = at(0, 1 - core)
    partner = at(group, core)
    across = at(group, 1 - core)

    barrier = pltpu.get_barrier_semaphore()
    for other in (ring_dev[0], ring_dev[1], twin, partner, across):
        pl.semaphore_signal(barrier, inc=1, device_id=other, device_id_type=MESH)

    def greet(step, _):
        pl.semaphore_signal(
            barrier, inc=1, device_id={"seq": lax.rem(row + step, nseq)}, device_id_type=MESH)
        return 0

    lax.fori_loop(1, nseq, greet, 0)

    def remote(src, dst, send, recv, device):
        return pltpu.make_async_remote_copy(
            src_ref=src, dst_ref=dst, send_sem=send, recv_sem=recv, device_id=device, device_id_type=MESH)

    def slot_of(side, r, h):
        j = (way[side] * h - r) % nz
        return slot_order.index(group - 1 - j) if j < group else None

    def source_block(side, h, c):
        return 2 * lax.rem(z - way[side] * h + 2 * nz, nz) + c

    def slot_rows(k):
        return pl.ds(k * sub, sub)

    relays = [[item for item in lists[side] if slot_of(side, *item) is None] for side in (0, 1)]

    def place_of(side, r, h, block):
        k = slot_of(side, r, h)
        if k is None:
            return relay.at[side, relays[side].index((r, h))]
        return x_buf.at[block, slot_rows(k)]

    def own_rows(r):
        q = lax.rem(z + r, nz)
        return pl.ds(pl.multiple_of(q * sub, sub), sub)

    def ring_copy(side, r, h):
        block = source_block(side, h - 1, core)
        src = tokens.at[own_rows(r)] if h == 1 else place_of(side, r, h - 1, block)
        n = index[side][(r, h)]
        return remote(src, place_of(side, r, h, block), ring_out.at[side, n], ring_in.at[side, n], ring_dev[side])

    def pair_copy(side, r, h, from_twin=False):
        block = source_block(side, h, 1 - core if from_twin else core)
        ref = place_of(side, r, h, block)
        n = index[side][(r, h)]
        return remote(ref, ref, pair_out.at[side, n], pair_in.at[side, n], twin)

    own_parts = [r for r in range(nz) if (-r) % nz < group]

    def own_slot(r):
        return slot_order.index(group - 1 - (-r) % nz)

    def own_load(n):
        r = own_parts[n]
        return pltpu.make_async_copy(
            tokens.at[own_rows(r)], x_buf.at[chan, slot_rows(own_slot(r))], local.at[n])

    def own_pair(n):
        r = own_parts[n]
        return remote(
            tokens.at[own_rows(r)], x_buf.at[chan, slot_rows(own_slot(r))], own_out.at[n], own_in.at[n], twin)

    wi_load = pltpu.make_async_copy(w_in, wi_a, local.at[group])

    far_wi = remote(w_in.at[row], wi_b.at[x, y], far_out.at[0], far_in.at[0], partner)

    def far_wo(c):
        cols = pl.ds(pl.multiple_of((2 * (row // 2) + c) * width, LANES), width)
        device = {"chan": 2 * lax.rem(z + group, nz) + c}
        return remote(w_out.at[:, cols], wo_b.at[x, y], far_out.at[1 + c], far_in.at[1], device)

    low_rows, high_rows = pl.ds(0, width // 2), pl.ds(width // 2, width // 2)

    def lines(which):
        buf = (wi_b, wo_b)[which]
        copies = []
        for step in range(1, NX):
            n = (step - 1, which)
            device = {"seq": lax.rem(x + step, NX) * ny + y}
            ref = buf.at[x, y, low_rows]
            copies.append(remote(ref, ref, line_out.at[n], line_in.at[n], device))
        for step in range(1, ny):
            n = (NX - 1 + step - 1, which)
            device = {"seq": x * ny + lax.rem(y + step, ny)}
            ref = buf.at[x, y, high_rows]
            copies.append(remote(ref, ref, line_out.at[n], line_in.at[n], device))
        return copies

    def pass_on(which, axis, i):
        n, p = ((NX, x), (ny, y))[axis]
        p = lax.rem(p + n + (0, 0, 0, 0, -1, 1)[i], n)
        part_i, step = (0, 1, 1, 0, 0, 1)[i], (1, 1, -1, -1, 1, -1)[i]
        buf = (wi_b, wo_b)[which]
        if axis == 0:
            ref = buf.at[p, pl.ds(part_i * (ny // 2), ny // 2), high_rows]
            device = {"seq": lax.rem(x + step + NX, NX) * ny + y}
        else:
            ref = buf.at[pl.ds(part_i * (NX // 2), NX // 2), p, low_rows]
            device = {"seq": x * ny + lax.rem(y + step + ny, ny)}
        return remote(ref, ref, pass_out.at[which, axis, i], pass_in.at[which, axis, i], device)

    def pass_list(which, name):
        picks = {"own": (0, 2, 1, 3), "first": (0, 2), "on": (4, 5), "rest": (1, 3, 4, 5)}[name]
        short = {"own": (0, 1), "first": (), "on": (), "rest": (0, 1)}[name]
        return [
            pass_on(which, axis, i)
            for place in range(4) for axis in (0, 1)
            for i in ((picks if (NX, ny)[axis] == 4 else short)[place:place + 1])]

    params = [
        remote(src, dst, prm_out.at[n], prm_in.at[n], partner)
        for n, (src, dst) in enumerate(((residues_in, far_res), (decays_in, far_dec), (skip_in, far_skip)))]
    own_params = [
        pltpu.make_async_copy(src, dst, own_prm.at[n])
        for n, (src, dst) in enumerate(((residues_in, residues), (decays_in, decays), (skip_in, skip)))]

    def wo_cols(block, c):
        return pl.ds(pl.multiple_of((2 * block + c) * width, LANES), width)

    def wo_copy(block):
        return remote(
            w_out.at[:, wo_cols(block, 1 - core)], wo_a.at[block, pl.ds(core * width, width)],
            wo_sent.at[block], wo_in.at[block], twin)

    def wo_load(block):
        return pltpu.make_async_copy(
            w_out.at[:, wo_cols(block, core)], wo_a.at[block, pl.ds(core * width, width)],
            local.at[group + 1 + block])

    def half_rows(hf):
        return pl.ds(hf * half, half)

    def project(delta, hf, ab, first):
        total = None
        source = lax.rem(z - delta + nz, nz)
        for c in range(2):
            block = 2 * source + c
            weights = wi_a[block] if ab == 0 else wi_b[block // ny, lax.rem(block, ny)]
            term = jnp.dot(x_buf[block, half_rows(hf)], weights, preferred_element_type=F32)
            total = term if total is None else total + term
        if first:
            acc[ab, half_rows(hf)] = total
        else:
            acc[ab, half_rows(hf)] += total

    cut = jnp.where(low_chip, group - 1 - z, 0)
    sub_id = lax.broadcasted_iota(jnp.int32, (SUB, LANES), 0)
    in_slot = sub_id % seg
    tiles = width // LANES

    def combine(terms):
        while len(terms) > 1:
            terms = [terms[k] + terms[k + 1] if k + 1 < len(terms) else terms[k] for k in range(0, len(terms), 2)]
        return terms[0]

    def scan(turn, tile, hf):
        lanes = pl.ds(tile * LANES, LANES)
        spot = turn * tiles + tile
        ab = jnp.where(low_chip, turn, 1 - turn)
        u_buf[spot, half_rows(hf)] = acc[ab, half_rows(hf), lanes].astype(BF16).astype(F32)
        a = [jnp.broadcast_to(jnp.exp(-d_buf[turn, r:r + 1, lanes]), (SUB, LANES)) for r in range(order)]
        g = [jnp.broadcast_to(g_buf[turn, r:r + 1, lanes], (SUB, LANES)) for r in range(order)]
        direct = jnp.broadcast_to(k_buf[turn, :, lanes], (SUB, LANES))

        def body(i, hs):
            where = pl.ds(hf * half + i, SUB, stride=span)
            u = u_buf[spot, where]
            hs = tuple(a[r] * hs[r] + g[r] * u for r in range(order))
            u_buf[spot, where] = combine([direct * u] + list(hs))
            return hs

        hs = lax.fori_loop(
            0, span, body, tuple(jnp.zeros((SUB, LANES), F32) for _ in range(order)), unroll=UNROLL)
        for r in range(order):
            run = hs[r]
            for shift in (1, 2, 4):
                if shift < seg:
                    factor = jnp.exp(-d_buf[turn, r:r + 1, lanes] * float(span * shift))
                    run = run + jnp.where(in_slot >= shift, factor * pltpu.roll(run, shift, 0), 0.0)
            before[turn, hf, r, :, lanes] = jnp.where(in_slot >= 1, pltpu.roll(run, 1, 0), 0.0)
            for n in range(per_half):
                k = slot_order[hf * per_half + n]
                slot_end[turn, k, r:r + 1, lanes] = run[(n + 1) * seg - 1:(n + 1) * seg]

    early = [(turn, tile) for turn in range(2) for tile in range(tiles)]

    for n in range(group):
        own_load(n).start()
    wi_load.start()
    for copy in own_params:
        copy.start()
    pl.semaphore_wait(barrier, nseq + 4)
    far_wi.start()
    for side in (0, 1):
        ring_copy(side, *lists[side][0]).start()
    for n in range(group):
        own_pair(n).start()

    sources = {}
    for side in (0, 1):
        for n, (r, h) in enumerate(lists[side]):
            if slot_of(side, r, h) is not None:
                sources.setdefault(((way[side] * h) % nz, slot_of(side, r, h) // per_half), []).append((side, r, h, n))
    whole = {key: max(n for _, _, _, n in got) + LAG + 1 for key, got in sources.items()}

    arrived_items, fresh = set(), []

    def arrive(side, r, h):
        if (side, r, h) not in arrived_items:
            arrived_items.add((side, r, h))
            fresh.append((side, r, h))
            ring_copy(side, r, h).wait_recv()

    def hook(place):
        if place == WO_START:
            @pl.when(core == lax.rem(row, 2))
            def _():
                for c in range(2):
                    far_wo(c).start()
        if place == WO_FIRST:
            far_wo(0).wait_recv()
            for copy in lines(1):
                copy.start()
        if place == WO_SECOND:
            for copy in lines(1):
                copy.wait_recv()
            for copy in pass_list(1, "own"):
                copy.start()
        if place == WO_RELAY:
            for copy in pass_list(1, "first"):
                copy.wait_recv()
            for copy in pass_list(1, "on"):
                copy.start()

    far_ready = False
    projected = []
    for step in range(max(count + LAG + 2, WI_DONE + 1)):
        for side in (0, 1):
            if 0 < step < count:
                r, h = lists[side][step]
                if h > 1:
                    arrive(side, r, h - 1)
                ring_copy(side, r, h).start()
        for side in (0, 1):
            if LAG <= step < count + LAG:
                arrive(side, *lists[side][step - LAG])
            for item in list(fresh):
                fresh.remove(item)
                if slot_of(*item) is not None:
                    pair_copy(*item).start()
        if step == 1:
            for copy in params:
                copy.start()
        if step == 6:
            for block in range(nz):
                wo_load(block).start()
                wo_copy(block).start()
        if step == 2:
            for n in range(group):
                own_load(n).wait()
                own_pair(n).wait_recv()
            wi_load.wait()
            for hf in range(2):
                project(0, hf, 0, True)
                projected.append((0, hf))
        hook(step)
        if step == WI_FIRST:
            far_wi.wait_recv()
            for copy in lines(0):
                copy.start()
        if step == WI_SECOND:
            for copy in lines(0):
                copy.wait_recv()
            for copy in pass_list(0, "own"):
                copy.start()
        if step == WI_RELAY:
            for copy in pass_list(0, "first"):
                copy.wait_recv()
            for copy in pass_list(0, "on"):
                copy.start()
        if step == WI_DONE:
            for copy in pass_list(0, "rest"):
                copy.wait_recv()
            far_ready = True
            for delta, hf in projected:
                project(delta, hf, 1, delta == 0)
            for copy in params:
                copy.wait_recv()
            for copy in own_params:
                copy.wait()
            g_buf[near] = residues[...] * jnp.sqrt(decays[...])
            g_buf[1 - near] = far_res[...] * jnp.sqrt(far_dec[...])
            d_buf[near] = decays[...]
            d_buf[1 - near] = far_dec[...]
            k_buf[near] = skip[...]
            k_buf[1 - near] = far_skip[...]
        for key, ready in whole.items():
            if ready == step:
                for side, r, h, _ in sources[key]:
                    pair_copy(side, r, h, True).wait_recv()
                project(*key, 0, False)
                if far_ready:
                    project(*key, 1, False)
                projected.append(key)
        if far_ready and len([1 for _, hf in projected if hf == 0]) == nz and early:
            scan(*early.pop(0), 0)
    assert far_ready and len(projected) == 2 * nz
    for turn, tile in early:
        scan(turn, tile, 0)

    def decay_over(turn, parts):
        return jnp.exp(-d_buf[turn] * (parts * sub).astype(F32))

    def state_copy(turn, src, target):
        return remote(
            states.at[turn, src], states.at[turn, src], state_out.at[turn, target], state_in.at[turn, src],
            {"seq": target})

    def join_last(turn):
        return remote(last.at[turn], pair_last.at[turn], join_out.at[turn, 0], join_in.at[turn, 0], partner)

    def join_carry(turn):
        return remote(
            carries.at[turn, 0], carries.at[turn, 1], join_out.at[turn, 1], join_in.at[turn, 1], partner)

    for turn in range(2):
        hook(100 + turn)
        for tile in range(tiles):
            scan(turn, tile, 1)
        slot_decay = jnp.exp(-d_buf[turn] * float(sub))
        run = tail = jnp.zeros((order, width), F32)
        for k in range(group):
            run = jnp.where(cut == k, 0.0, run * slot_decay) + slot_end[turn, k]
            tail = jnp.where(cut == k + 1, run, tail)
        last[turn] = run
        states[turn, row] = decay_over(turn, nz - 1 - z) * run + tail

        def send_state(target, _, turn=turn):
            state_copy(turn, row, target).start()
            return 0

        lax.fori_loop(row + 1, nseq, send_state, 0)
        join_last(turn).start()

    def get_carry(turn):
        block_decay = jnp.exp(-d_buf[turn] * float(rows))

        def add_state(src, carry):
            state_copy(turn, src, row).wait_recv()
            return block_decay * carry + states[turn, src]

        carries[turn, 0] = lax.fori_loop(0, row, add_state, jnp.zeros((order, width), F32))
        join_carry(turn).start()

    def set_powers(turn):
        for tile in range(tiles):
            lanes = pl.ds(tile * LANES, LANES)
            for r in range(order):
                power[turn, r, :, lanes] = jnp.exp(
                    -d_buf[turn, r:r + 1, lanes] * (in_slot.astype(F32) * float(span)))

    def join(turn):
        to_middle = decay_over(turn, jnp.where(low_chip, z + 1, z - group + 1))
        to_end = jnp.exp(-d_buf[turn] * float(group * sub))
        join_last(turn).wait_recv()
        join_carry(turn).wait_recv()
        carry = carries[turn, 0] + carries[turn, 1]
        middle = to_middle * carry + jnp.where(low_chip, last[turn], pair_last[turn])
        begin = jnp.where(low_chip, carry, middle)
        slot_decay = jnp.exp(-d_buf[turn] * float(sub))
        ahead = jnp.where(cut > 0, to_end * middle + pair_last[turn], begin)
        for k in range(group):
            if k > 0:
                ahead = jnp.where(cut == k, begin, ahead * slot_decay + slot_end[turn, k - 1])
            slot_start[turn, k] = ahead

    def finish(turn, tile, hf):
        lanes = pl.ds(tile * LANES, LANES)
        spot = turn * tiles + tile
        a = [jnp.broadcast_to(jnp.exp(-d_buf[turn, r:r + 1, lanes]), (SUB, LANES)) for r in range(order)]
        hs = []
        for r in range(order):
            start = None
            for n in range(per_half):
                value = slot_start[turn, slot_order[hf * per_half + n], r:r + 1, lanes]
                start = value if start is None else jnp.where(sub_id >= n * seg, value, start)
            hs.append(before[turn, hf, r, :, lanes] + power[turn, r, :, lanes] * start)

        def body(i, hs):
            where = pl.ds(hf * half + i, SUB, stride=span)
            hs = tuple(a[r] * hs[r] for r in range(order))
            u_buf[spot, where] = combine([u_buf[spot, where]] + list(hs))
            return hs

        lax.fori_loop(0, span, body, tuple(hs), unroll=UNROLL)
        conv[core, turn, half_rows(hf), lanes] = u_buf[spot, half_rows(hf)].astype(BF16)

    def conv_copy(turn, hf, c):
        ref = conv.at[c, turn, half_rows(hf)]
        return remote(ref, ref, conv_out.at[turn, hf], conv_in.at[turn, hf], twin)

    for turn in range(2):
        hook(102 + turn)
        set_powers(turn)
    for turn in range(2):
        get_carry(turn)
        hook(104 + turn)
    for turn in range(2):
        join(turn)
        for hf in (0, 1):
            for tile in range(tiles):
                finish(turn, tile, hf)
            conv_copy(turn, hf, core).start()

    def part_terms(delta, hf, c):
        block = lax.rem(z - delta + nz, nz)
        share = 2 * block + c
        return jnp.dot(
            conv[c, near, half_rows(hf)], wo_a[block, pl.ds(c * width, width)], preferred_element_type=F32) + jnp.dot(
            conv[c, 1 - near, half_rows(hf)], wo_b[share // ny, lax.rem(share, ny)], preferred_element_type=F32)

    for block in range(nz):
        wo_load(block).wait()
        wo_copy(block).wait_recv()
    for copy in pass_list(1, "rest"):
        copy.wait_recv()

    def target_of(side, r, i):
        length = (up, down)[side][r]
        h = length - i + 1
        return (way[side] * h) % nz, slot_of(side, r, h)

    def sum_copy(side, r, i):
        n = sum_index[side][(r, i)]
        delta, k = target_of(side, r, i)
        src = arrived.at[side, sum_index[side][(r, i - 1)]] if k is None else leaving.at[side, n]
        return remote(src, arrived.at[side, n], sum_out.at[side, n], sum_in.at[side, n], ring_dev[1 - side])

    have, seen = set(), set()

    def need(delta, k):
        hf = k // per_half
        if hf not in seen:
            seen.add(hf)
            for turn in range(2):
                conv_copy(turn, hf, 1 - core).wait_recv()
        if (delta, hf) not in have:
            have.add((delta, hf))
            part[delta, half_rows(hf)] = part_terms(delta, hf, 0) + part_terms(delta, hf, 1)

    def out_copy(r):
        return pltpu.make_async_copy(result.at[r], out.at[own_rows(r)], out_sem.at[r])

    def finish_sum(r):
        total = None
        if (-r) % nz < group:
            need(0, own_slot(r))
            total = part[0, slot_rows(own_slot(r))]
        for side in (0, 1):
            length = (up, down)[side][r]
            if length > 0:
                sum_copy(side, r, length).wait_recv()
                got = arrived[side, sum_index[side][(r, length)]].astype(F32)
                total = got if total is None else total + got
        result[r] = total.astype(BF16)
        out_copy(r).start()

    drains = []
    for side in (0, 1):
        for item in lists[side]:
            drains.append(ring_copy(side, *item).wait_send)
            if slot_of(side, *item) is not None:
                drains.append(pair_copy(side, *item).wait_send)
    drains += [own_pair(n).wait_send for n in range(group)] + [far_wi.wait_send]
    for which in range(2):
        drains += [copy.wait_send for copy in lines(which) + pass_list(which, "own") + pass_list(which, "on")]
    drains += [copy.wait_send for copy in params]
    drains += [wo_copy(block).wait_send for block in range(nz)]
    for turn in range(2):
        drains += [join_last(turn).wait_send, join_carry(turn).wait_send]
        drains += [conv_copy(turn, hf, core).wait_send for hf in range(2)]

    def drain_far():
        @pl.when(core == lax.rem(row, 2))
        def _():
            for c in range(2):
                far_wo(c).wait_send()

    def drain_states():
        def one(target, _):
            for turn in range(2):
                state_copy(turn, row, target).wait_send()
            return 0

        lax.fori_loop(row + 1, nseq, one, 0)

    drains += [drain_far, drain_states]
    batch = -(-len(drains) // (count - 2))

    ends = {r: max([sum_index[s][(r, (up, down)[s][r])] for s in (0, 1) if (up, down)[s][r] > 0] + [0]) + SUM_LAG for r in range(nz)}
    for step in range(count + SUM_LAG + 1):
        for side in (0, 1):
            if step < count:
                r, i = sum_lists[side][step]
                delta, k = target_of(side, r, i)
                if k is not None:
                    need(delta, k)
                if i > 1:
                    sum_copy(side, r, i - 1).wait_recv()
                if k is not None:
                    value = part[delta, slot_rows(k)]
                    if i > 1:
                        value = value + arrived[side, sum_index[side][(r, i - 1)]].astype(F32)
                    leaving[side, sum_index[side][(r, i)]] = value.astype(BF16)
                sum_copy(side, r, i).start()
        if step > 0:
            for wait in drains[:batch]:
                wait()
            del drains[:batch]
        for r in range(nz):
            if ends[r] == step:
                finish_sum(r)

    for side in (0, 1):
        for item in sum_lists[side]:
            sum_copy(side, *item).wait_send()
    for r in range(nz):
        out_copy(r).wait()
    assert not drains


def per_device(nseq, nchan, tokens, w_in, residues, decays, skip_gain, w_out):
    rows, width = tokens.shape
    order = residues.shape[1]
    nz = nchan // 2
    ny = nseq // NX
    group = nz // 2
    mine = rows // 2
    count = len(paths(nz, LAG)[2][0])
    dma = pltpu.SemaphoreType.DMA
    hbm = pl.BlockSpec(memory_space=pl.ANY)
    flops = 4 * rows * width * nchan * width
    return pl.pallas_call(
        functools.partial(kernel, nseq, nz, rows, width, order),
        out_shape=jax.ShapeDtypeStruct((rows, width), BF16),
        in_specs=[hbm] * 6,
        out_specs=hbm,
        scratch_shapes=[
            pltpu.VMEM((nchan, mine, width), BF16),
            pltpu.VMEM((2, 1, rows // nz, width), BF16),
            pltpu.VMEM((nz, rows // nz, width), BF16),
            pltpu.VMEM((nchan, width, width), BF16),
            pltpu.VMEM((NX, ny, width, width), BF16),
            pltpu.VMEM((nz, 2 * width, width), BF16),
            pltpu.VMEM((NX, ny, width, width), BF16),
            pltpu.VMEM((2, mine, width), F32),
            pltpu.VMEM((2 * width // LANES, mine, LANES), F32),
            pltpu.VMEM((2, 2, mine, width), BF16),
            pltpu.VMEM((nz, mine, width), F32),
            pltpu.VMEM((2, count, rows // nz, width), BF16),
            pltpu.VMEM((2, count, rows // nz, width), BF16),
            pltpu.VMEM((order, width), F32),
            pltpu.VMEM((order, width), F32),
            pltpu.VMEM((1, width), F32),
            pltpu.VMEM((order, width), F32),
            pltpu.VMEM((order, width), F32),
            pltpu.VMEM((1, width), F32),
            pltpu.VMEM((2, order, width), F32),
            pltpu.VMEM((2, order, width), F32),
            pltpu.VMEM((2, 1, width), F32),
            pltpu.VMEM((2, order, SUB, width), F32),
            pltpu.VMEM((2, 2, order, SUB, width), F32),
            pltpu.VMEM((2, group, order, width), F32),
            pltpu.VMEM((2, group, order, width), F32),
            pltpu.VMEM((2, order, width), F32),
            pltpu.VMEM((2, nseq, order, width), F32),
            pltpu.VMEM((2, 2, order, width), F32),
            pltpu.VMEM((2, order, width), F32),
            dma((2, count)), dma((2, count)),
            dma((2, count)), dma((2, count)),
            dma((group,)), dma((group,)),
            dma((2, count)), dma((2, count)),
            dma((2, nseq)), dma((2, nseq)),
            dma((2, 2)), dma((2, 2)),
            dma((nz,)), dma((nz,)),
            dma((2,)), dma((3,)),
            dma((NX + ny - 2, 2)), dma((NX + ny - 2, 2)),
            dma((2, 2, 6)), dma((2, 2, 6)),
            dma((3,)), dma((3,)),
            dma((2, 2)), dma((2, 2)),
            dma((group + 1 + nz,)),
            dma((3,)),
            dma((nz,)),
        ],
        compiler_params=pltpu.CompilerParams(
            collective_id=0, has_side_effects=True, vmem_limit_bytes=56 * 1024 * 1024),
        cost_estimate=pl.CostEstimate(flops=flops, bytes_accessed=6 * 1024 * 1024, transcendentals=0),
    )(tokens, w_in.reshape(nchan, width, width), residues.T, decays.T, skip_gain.reshape(1, width), w_out)


def solution(mesh):
    in_specs = (
        P("seq", "chan"),
        P(None, "chan"),
        P("chan", None),
        P("chan", None),
        P("chan"),
        P("chan", None),
    )
    return jax.shard_map(
        functools.partial(per_device, mesh.shape["seq"], mesh.shape["chan"]),
        mesh=mesh, in_specs=in_specs, out_specs=P("seq", "chan"), check_vma=False)
```
